256 devices in a mesh: row: 16 (over z_hi, x), col: 16 (over z_lo, y, core).
Axes of the slice: x: 4, y: 4, z: 8 (z_hi: 4, z_lo: 2; z = z_hi * 2 + z_lo), core: 2. Of those that a mesh axis runs over, the one named last changes fastest.
Arguments:
- alignment: bfloat16 [512, 384, 256], P('row', 'col'), may hold values from -8 to 8
- alignment_mask: int32 [512, 384], P('row', 'col'), may hold values from 0 to 1, as said below
- residue_mask: int32 [384], replicated, may hold values from 0 to 1, as said below
- pair_features: bfloat16 [384, 384, 128], P('row', 'col'), may hold values from -6 to 6
- outer_product_left: bfloat16 [256, 32], replicated, may hold values from -0.375 to 0.375
- outer_product_right: bfloat16 [256, 32], replicated, may hold values from -0.375 to 0.375
- outer_proj: bfloat16 [1024, 128], replicated, may hold values from -0.1875 to 0.1875
- triangle_proj: bfloat16 [128, 512], replicated, may hold values from -0.5 to 0.5
- triangle_gate: bfloat16 [128, 128], replicated, may hold values from -0.5 to 0.5
- triangle_out: bfloat16 [128, 128], replicated, may hold values from -0.5 to 0.5
- transition_in: bfloat16 [128, 512], replicated, may hold values from -0.5 to 0.5
- transition_out: bfloat16 [512, 128], replicated, may hold values from -0.25 to 0.25
Outputs:
- pair_out: bfloat16 [384, 384, 128], P('row', 'col')
The draws below stay inside these ranges and needn't reach their ends.
Inputs may be any that keep to these rules, and one draw needn't show every extreme that they name: `residue_mask`: masked residues scattered anywhere; at least one residue is masked and at least one takes part. `alignment_mask`: 0 wherever residue_mask is 0.
All inputs are finite; a program needn't handle non-finite values.
Results may differ from the reference program's by a relative error of at most 0.014.
Values may be sent and summed in bfloat16 or wider, within the bound.
A program may use at most 64 MiB of HBM per device.

```python
import jax
import jax.numpy as jnp
from jax import lax

ALIGN_CHANNELS = 256
PAIR_WIDTH = 128
OUTER_CHANNELS = 32
TRI_WIDTH = 128
TRANS_WIDTH = 512
RES_ROW = 24
SEQUENCE_COUNT = 512
RESIDUE_COUNT = 384
N_ROW = 16


def masks_together(key):
    residue_flips = jax.random.randint(jax.random.fold_in(key, 7), (RESIDUE_COUNT,), 0, 8)
    residue_part = (residue_flips < 7).astype(jnp.int32)
    zero_place = jax.random.randint(jax.random.fold_in(key, 13), (), 0, RESIDUE_COUNT)
    offset_place = jax.random.randint(jax.random.fold_in(key, 17), (), 1, RESIDUE_COUNT)
    one_place = (zero_place + offset_place) % RESIDUE_COUNT
    positions = jnp.arange(RESIDUE_COUNT, dtype=jnp.int32)
    residue_part = jnp.where(positions == one_place, jnp.int32(1), residue_part)
    residue_part = jnp.where(positions == zero_place, jnp.int32(0), residue_part).astype(jnp.int32)
    coin_flips = jax.random.randint(jax.random.fold_in(key, 11), (SEQUENCE_COUNT, RESIDUE_COUNT), 0, 20)
    present = (coin_flips < 17).astype(jnp.int32) * residue_part[None, :]
    return (residue_part, present)


def draw_residue_mask(key, part):
    return masks_together(key)[0]


def draw_alignment_mask(key, part):
    return masks_together(key)[1]


def draw_alignment(key, part):
    sequence_profile = jax.random.normal(jax.random.fold_in(key, 1), (1, RESIDUE_COUNT, ALIGN_CHANNELS), jnp.float32)
    random_jitter = jax.random.normal(jax.random.fold_in(key, 2), (SEQUENCE_COUNT, RESIDUE_COUNT, ALIGN_CHANNELS), jnp.float32)
    values = 0.8 * sequence_profile + 0.7 * random_jitter
    return jnp.clip(values, -8.0, 8.0).astype(jnp.bfloat16)


def levels(rng, shape, pieces, least, largest):
    factor_of, own = 1.0, jax.random.fold_in(rng, 6)
    for dim, blocks in pieces:
        heights = jnp.exp(jax.random.uniform(jax.random.fold_in(own, dim), (blocks,), jnp.float32, least / len(pieces), largest / len(pieces)))
        factor_of = factor_of * jnp.repeat(heights, shape[dim] // blocks).reshape([-1 if axis == dim else 1 for axis in range(len(shape))])
    return factor_of


def gaussian(own_key, shape, deviation, reach, cuts=(), held_as=jnp.bfloat16):
    array = jax.random.normal(own_key, shape, jnp.float32) * deviation
    if len(cuts) > 0:
        array = levels(own_key, shape, cuts, -0.22, 0.18) * array
    return jnp.clip(array, min=-reach, max=reach).astype(held_as)


def setup_inputs(seed: int = 0) -> dict:
    arg_keys = jax.random.split(jax.random.key(seed), 13)
    alignment = draw_alignment(jax.random.fold_in(arg_keys[12], 71), 0)
    alignment_mask = draw_alignment_mask(jax.random.fold_in(arg_keys[12], 71), 0)
    residue_mask = draw_residue_mask(jax.random.fold_in(arg_keys[12], 71), 0)
    pair_features = gaussian(arg_keys[3], (RESIDUE_COUNT, RESIDUE_COUNT, PAIR_WIDTH), 1.0, 6.0, ((0, 16), (1, 16)))
    outer_product_left = gaussian(arg_keys[4], (ALIGN_CHANNELS, OUTER_CHANNELS), ALIGN_CHANNELS ** -0.5, 0.375)
    outer_product_right = gaussian(arg_keys[5], (ALIGN_CHANNELS, OUTER_CHANNELS), ALIGN_CHANNELS ** -0.5, 0.375)
    outer_proj = gaussian(arg_keys[6], (OUTER_CHANNELS * OUTER_CHANNELS, PAIR_WIDTH), (OUTER_CHANNELS * OUTER_CHANNELS) ** -0.5, 0.1875)
    triangle_proj = gaussian(arg_keys[7], (PAIR_WIDTH, 4 * TRI_WIDTH), PAIR_WIDTH ** -0.5, 0.5)
    triangle_gate = gaussian(arg_keys[8], (PAIR_WIDTH, PAIR_WIDTH), PAIR_WIDTH ** -0.5, 0.5)
    triangle_out = gaussian(arg_keys[9], (TRI_WIDTH, PAIR_WIDTH), TRI_WIDTH ** -0.5, 0.5)
    transition_in = gaussian(arg_keys[10], (PAIR_WIDTH, TRANS_WIDTH), PAIR_WIDTH ** -0.5, 0.5)
    transition_out = gaussian(arg_keys[11], (TRANS_WIDTH, PAIR_WIDTH), TRANS_WIDTH ** -0.5, 0.25)
    return {"alignment": alignment, "alignment_mask": alignment_mask, "residue_mask": residue_mask, "pair_features": pair_features, "outer_product_left": outer_product_left, "outer_product_right": outer_product_right, "outer_proj": outer_proj, "triangle_proj": triangle_proj, "triangle_gate": triangle_gate, "triangle_out": triangle_out, "transition_in": transition_in, "transition_out": transition_out}


epsilon = 1e-05

def normalize(values):
    mean_value = lax.optimization_barrier(jnp.mean(values, axis=-1, keepdims=True))
    centered = values - mean_value
    variance = lax.optimization_barrier(jnp.mean(centered * centered, axis=-1, keepdims=True))
    return centered * lax.rsqrt(variance + epsilon)

def reference(alignment, alignment_mask, residue_mask, pair_features, outer_product_left, outer_product_right, outer_proj, triangle_proj, triangle_gate, triangle_out, transition_in, transition_out):
    mask_float = alignment_mask.astype(jnp.float32)
    normed = normalize(alignment.astype(jnp.float32)).astype(jnp.bfloat16)
    left_side = (jnp.dot(normed, outer_product_left, preferred_element_type=jnp.float32) * mask_float[..., None]).astype(jnp.bfloat16)
    right_side = (jnp.dot(normed, outer_product_right, preferred_element_type=jnp.float32) * mask_float[..., None]).astype(jnp.bfloat16)
    counts = jnp.dot(mask_float.T, mask_float, precision=lax.Precision.HIGHEST)
    right_float = right_side.astype(jnp.float32)

    def outer_rows(first_row):
        left_block = lax.dynamic_slice_in_dim(left_side, first_row, RES_ROW, 1).astype(jnp.float32)
        outer = jnp.einsum('sic,sjd->ijcd', left_block, right_float, precision=lax.Precision.HIGHEST)
        outer = outer.astype(jnp.bfloat16).reshape(RES_ROW, RESIDUE_COUNT, OUTER_CHANNELS * OUTER_CHANNELS)
        return jnp.dot(outer, outer_proj, preferred_element_type=jnp.float32)
    row_starts = jnp.arange(N_ROW, dtype=jnp.int32) * RES_ROW
    projected = lax.map(outer_rows, row_starts).reshape(RESIDUE_COUNT, RESIDUE_COUNT, PAIR_WIDTH)
    first = (pair_features.astype(jnp.float32) + projected / jnp.maximum(counts, 1.0)[..., None]).astype(jnp.bfloat16)
    normed_pair = normalize(first.astype(jnp.float32)).astype(jnp.bfloat16)
    projections = jnp.dot(normed_pair, triangle_proj, preferred_element_type=jnp.float32)
    residue_float = residue_mask.astype(jnp.float32)
    pair_mask = (residue_float[:, None] * residue_float[None, :])[..., None]
    width = TRI_WIDTH
    left_tri = (jax.nn.sigmoid(projections[..., :width]) * projections[..., width:2 * width] * pair_mask).astype(jnp.bfloat16)
    right_tri = (jax.nn.sigmoid(projections[..., 2 * width:3 * width]) * projections[..., 3 * width:] * pair_mask).astype(jnp.bfloat16)
    summed = jnp.einsum('ikc,jkc->ijc', left_tri.astype(jnp.float32), right_tri.astype(jnp.float32), precision=lax.Precision.HIGHEST)
    normed_sum = normalize(summed).astype(jnp.bfloat16)
    update = jax.nn.sigmoid(jnp.dot(normed_pair, triangle_gate, preferred_element_type=jnp.float32)) * jnp.dot(normed_sum, triangle_out, preferred_element_type=jnp.float32)
    second = (first.astype(jnp.float32) + update).astype(jnp.bfloat16)
    normed_second = normalize(second.astype(jnp.float32)).astype(jnp.bfloat16)
    hidden_units = jnp.maximum(jnp.dot(normed_second, transition_in, preferred_element_type=jnp.float32), 0.0).astype(jnp.bfloat16)
    return (second.astype(jnp.float32) + jnp.dot(hidden_units, transition_out, preferred_element_type=jnp.float32)).astype(jnp.bfloat16)
```

```python
import jax
import jax.numpy as jnp
from jax import lax
from jax.experimental import pallas as pl
from jax.experimental.pallas import tpu as pltpu
from jax.sharding import PartitionSpec as P

EPSILON = 1e-05
MESH = pl.DeviceIdType.MESH
F32 = jnp.float32
BF16 = jnp.bfloat16
I32 = jnp.int32

LEFT_SCATTER = 0
LEFT_GATHER = 16
RIGHT_GATHER = 33
TRI_SCATTER = 53
TRI_LEFT = 57
TRI_RIGHT = 74
TRANSFERS = 94


def norm(v):
    mean = jnp.mean(v, axis=-1, keepdims=True)
    centered = v - mean
    variance = jnp.mean(centered * centered, axis=-1, keepdims=True)
    return centered * lax.rsqrt(variance + EPSILON)


def dot(a, b):
    return jnp.dot(a, b, preferred_element_type=F32)


def kernel(
    align_ref, amask_ref, rmask_ref, pair_ref, wl_ref, wr_ref, oproj_ref, tproj_ref, tgate_ref,
    tout_ref, tin_ref, trans_ref, out_ref,
    xs, wbd, perm, bd, lnat, left_send, left_all, right_all, left_t, lhs2, pairf, first, normed,
    pmask, proj, gate, tri_left, tri_send, tri_right, rf, summed, ss, rs,
):
    r, q = lax.axis_index("row"), lax.axis_index("col")
    z, x = r // 4, lax.rem(r, 4)
    zl, y, core = q // 8, lax.rem(q // 2, 4), lax.rem(q, 2)
    same = r == q

    def row_of(zz, xx):
        return lax.rem(zz + 4, 4) * 4 + lax.rem(xx + 4, 4)

    def col_of(ll, yy, cc):
        return (ll * 4 + lax.rem(yy + 4, 4)) * 2 + cc

    zp, zm = (row_of(z + 1, x), q), (row_of(z - 1, x), q)
    xp, xm = (row_of(z, x + 1), q), (row_of(z, x - 1), q)
    yp, ym = (r, col_of(zl, y + 1, core)), (r, col_of(zl, y - 1, core))
    zlo = (r, col_of(1 - zl, y, core))
    twin = (r, col_of(zl, y, 1 - core))

    barrier = pltpu.get_barrier_semaphore()
    for device in (zp, zm, xp, xm, yp, ym, zlo, twin):
        pl.semaphore_signal(barrier, inc=1, device_id=device, device_id_type=MESH)

    def greet(t, carry):
        @pl.when(jnp.logical_not(same & (t == r)))
        def _():
            pl.semaphore_signal(barrier, inc=1, device_id=(t, r), device_id_type=MESH)

        return carry

    lax.fori_loop(0, 16, greet, 0)

    def greet_tri(t, carry):
        @pl.when(jnp.logical_not(same & (t * 4 + x == q)))
        def _():
            pl.semaphore_signal(barrier, inc=1, device_id=(q, t * 4 + x), device_id_type=MESH)

        return carry

    lax.fori_loop(0, 4, greet_tri, 0)

    def norm_chunk(t, carry):
        rows = pl.ds(pl.multiple_of(t * 96, 96), 96)
        v = norm(align_ref[rows, :].astype(F32))
        xs[0, rows, :] = v[:, :128]
        xs[1, rows, :] = v[:, 128:]
        return carry

    lax.fori_loop(0, 8, norm_chunk, 0)

    lane = lax.broadcasted_iota(I32, (256, 128), 1)
    spread = (
        lax.rem(lax.broadcasted_iota(I32, (32, 128), 1), 32)
        == lax.broadcasted_iota(I32, (32, 128), 0)
    ).astype(F32).astype(BF16)
    for side, w_ref in enumerate((wl_ref, wr_ref)):
        w = dot(w_ref[...], spread)
        for u in range(4):
            own = (lane >= 32 * u) & (lane < 32 * u + 32)
            wbd[256 * u : 256 * u + 256, 128 * side : 128 * side + 128] = jnp.where(
                own, w, 0.0
            ).astype(BF16)

    lam = lax.broadcasted_iota(I32, (1, 768), 1)
    by24 = (lam * 2731) // 65536
    target = (lam - by24 * 24) * 32 + by24

    def perm_chunk(t, carry):
        start = pl.multiple_of(t * 64, 64)
        rows = lax.broadcasted_iota(I32, (64, 768), 0) + start
        perm[pl.ds(start, 64), :] = (rows == target).astype(F32).astype(BF16)
        return carry

    lax.fori_loop(0, 12, perm_chunk, 0)

    amask = amask_ref[...].astype(F32).astype(BF16)
    row24 = lax.broadcasted_iota(I32, (24, 768), 0) * 32
    lane24 = lax.broadcasted_iota(I32, (24, 768), 1)
    expand = ((lane24 >= row24) & (lane24 < row24 + 32)).astype(F32).astype(BF16)
    mask_wide = dot(amask, expand)
    mask_lanes = dot(
        amask,
        (
            lax.broadcasted_iota(I32, (24, 128), 0) == lax.broadcasted_iota(I32, (24, 128), 1)
        ).astype(F32).astype(BF16),
    ).astype(BF16)
    for g in range(6):
        four = jnp.concatenate(
            [
                xs[half, pl.ds(4 * g + u, 32, stride=24), :].astype(BF16)
                for u in range(4)
                for half in range(2)
            ],
            axis=1,
        )
        both = dot(four, wbd[...])
        m = mask_wide[:, 128 * g : 128 * g + 128]
        lnat[:, 128 * g : 128 * g + 128] = (both[:, :128] * m).astype(BF16)
        right = (both[:, 128:] * m).astype(BF16)
        for h in range(2):
            right_all[h, pl.ds(pl.multiple_of(r * 16, 16), 16), 128 * g : 128 * g + 128] = right[
                16 * h : 16 * h + 16
            ]
    left = dot(lnat[...], perm[...]).astype(BF16)
    for h in range(2):
        right_all[h, pl.ds(pl.multiple_of(r * 16, 16), 16), 768:896] = mask_lanes[
            16 * h : 16 * h + 16
        ]
        for g in range(6):
            left_send[8 * h + g] = left[16 * h : 16 * h + 16, 128 * g : 128 * g + 128]
        left_send[8 * h + 6] = mask_lanes[16 * h : 16 * h + 16]
        left_send[8 * h + 7] = jnp.zeros((16, 128), BF16)

    def remote(src, dst, send, recv, device):
        return pltpu.make_async_remote_copy(
            src_ref=src, dst_ref=dst, send_sem=ss.at[send], recv_sem=rs.at[recv],
            device_id=device, device_id_type=MESH,
        )

    def send(ref, k, device):
        remote(ref, ref, k, k, device).start()

    def wait_recv(ref, k):
        remote(ref, ref, k, k, twin).wait_recv()

    def wait_send(ref, k):
        remote(ref, ref, k, k, twin).wait_send()

    class Ring:
        def __init__(self, slot, half, at, plus, minus, k):
            self.slot, self.half, self.at = slot, half, at
            self.plus, self.minus, self.k = plus, minus, k

        def pos(self, d):
            return lax.rem(self.at + d + 4, 4)

        def start(self):
            send(self.slot(self.at), self.k, self.plus)
            send(self.slot(self.at), self.k + 1, self.minus)

        def from_minus(self):
            wait_recv(self.slot(self.pos(-1)), self.k)
            send(self.half(self.pos(-1), 0), self.k + 2, self.plus)

        def from_plus(self):
            wait_recv(self.slot(self.pos(1)), self.k + 1)
            send(self.half(self.pos(1), 1), self.k + 3, self.minus)

        def finish(self):
            wait_recv(self.half(self.pos(2), 0), self.k + 2)
            wait_recv(self.half(self.pos(2), 1), self.k + 3)

        def drain(self):
            wait_send(self.slot(self.at), self.k)
            wait_send(self.slot(self.at), self.k + 1)
            wait_send(self.half(self.pos(-1), 0), self.k + 2)
            wait_send(self.half(self.pos(1), 1), self.k + 3)

    class Columns:
        def __init__(self, ref, half_rows, k):
            self.ref, self.k = ref, k

            def slot(ll):
                return lambda yy: ref.at[col_of(ll, yy, core)]

            def half(ll):
                return lambda yy, h: ref.at[
                    col_of(ll, yy, core), pl.ds(h * half_rows, half_rows)
                ]

            self.rings = [
                Ring(slot(ll), half(ll), y, yp, ym, k + 1 + 4 * e)
                for e, ll in enumerate((zl, 1 - zl))
            ]
            self.passed = []

        def to_twin(self, ll, yy):
            n = len(self.passed)
            at = lax.rem(yy + 4, 4)
            self.passed.append((ll, at))
            send(self.ref.at[col_of(ll, at, core)], self.k + 9 + n, twin)

        def start(self):
            send(self.ref.at[q], self.k, zlo)
            self.rings[0].start()
            self.to_twin(zl, y)

        def other_half(self):
            wait_recv(self.ref.at[col_of(1 - zl, y, core)], self.k)
            self.rings[1].start()
            self.to_twin(1 - zl, y)

        def from_minus(self, e):
            self.rings[e].from_minus()
            self.to_twin((zl, 1 - zl)[e], y - 1)

        def from_plus(self, e):
            self.rings[e].from_plus()
            self.to_twin((zl, 1 - zl)[e], y + 1)

        def finish(self, e):
            self.rings[e].finish()
            self.to_twin((zl, 1 - zl)[e], y + 2)

        def finish_twin(self):
            for n, (ll, at) in enumerate(self.passed):
                wait_recv(self.ref.at[col_of(ll, at, 1 - core)], self.k + 9 + n)

        def drain(self):
            wait_send(self.ref.at[q], self.k)
            for ring in self.rings:
                ring.drain()
            for n, (ll, at) in enumerate(self.passed):
                wait_send(self.ref.at[col_of(ll, at, core)], self.k + 9 + n)

    class Rows:
        def __init__(self, block, half, k):
            self.zring = Ring(
                lambda zz: block(zz, x), lambda zz, h: half(zz, x, h), z, zp, zm, k
            )

            def slot(zz):
                return lambda xx: block(zz, xx)

            def part(zz):
                return lambda xx, h: half(zz, xx, h)

            self.order = [z, lax.rem(z + 3, 4), lax.rem(z + 1, 4), lax.rem(z + 2, 4)]
            self.xrings = [
                Ring(slot(zz), part(zz), x, xp, xm, k + 4 + 4 * e)
                for e, zz in enumerate(self.order)
            ]

        def start(self):
            self.zring.start()
            self.xrings[0].start()

        def z_neighbours(self):
            self.zring.from_minus()
            self.xrings[1].start()
            self.zring.from_plus()
            self.xrings[2].start()

        def z_far(self):
            self.zring.finish()
            self.xrings[3].start()

        def x_neighbours(self, e):
            self.xrings[e].from_minus()
            self.xrings[e].from_plus()

        def x_far(self, e):
            self.xrings[e].finish()

        def drain(self):
            self.zring.drain()
            for ring in self.xrings:
                ring.drain()

    def right_rows(zz, xx):
        return pl.ds(pl.multiple_of((zz * 4 + xx) * 16, 16), 16)

    right_rows_gather = Rows(
        lambda zz, xx: right_all.at[:, right_rows(zz, xx), :],
        lambda zz, xx, h: right_all.at[pl.ds(h, 1), right_rows(zz, xx), :],
        RIGHT_GATHER,
    )
    left_columns = Columns(left_all, 128, LEFT_GATHER)

    pl.semaphore_wait(barrier, 28 - 2 * same.astype(I32))

    right_rows_gather.start()
    own_rows = pl.ds(pl.multiple_of(r * 16, 16), 16)

    def scatter(t, carry):
        is_self = same & (t == q)

        @pl.when(jnp.logical_not(is_self))
        def _():
            remote(
                left_send.at[t], left_all.at[t, own_rows], LEFT_SCATTER + t, LEFT_SCATTER + r, (q, t)
            ).start()

        @pl.when(is_self)
        def _():
            left_all[t, own_rows] = left_send[t]

        return carry

    lax.fori_loop(0, 16, scatter, 0)

    def zero_chunk(t, carry):
        bd[pl.ds(pl.multiple_of(t * 128, 128), 128), :] = jnp.zeros((128, 512), BF16)
        return carry

    lax.fori_loop(0, 32, zero_chunk, 0)

    def fill_chunk(t, carry):
        block = oproj_ref[pl.ds(pl.multiple_of(t * 32, 32), 32), :]
        for u in range(4):
            bd[pl.ds(pl.multiple_of(t * 128 + 32 * u, 32), 32), 128 * u : 128 * u + 128] = block
        return carry

    lax.fori_loop(0, 32, fill_chunk, 0)

    def scatter_arrived(t, carry):
        @pl.when(jnp.logical_not(same & (t == r)))
        def _():
            piece = left_all.at[q, pl.ds(pl.multiple_of(t * 16, 16), 16)]
            remote(piece, piece, LEFT_SCATTER + t, LEFT_SCATTER + t, twin).wait_recv()

        return carry

    lax.fori_loop(0, 16, scatter_arrived, 0)
    left_columns.start()
    right_rows_gather.z_neighbours()
    left_columns.other_half()

    pairf[...] = pair_ref[...].astype(F32)
    mask_i = jnp.zeros((24, 128), F32)
    sub = lax.broadcasted_iota(I32, (24, 128), 0)
    for i in range(24):
        mask_i = jnp.where(sub == i, rmask_ref[r * 24 + i].astype(F32), mask_i)
    for k in range(24):
        pmask[24 * k : 24 * k + 24, :] = mask_i * rmask_ref[q * 24 + k].astype(F32)

    right_rows_gather.x_neighbours(0)
    left_columns.from_minus(0)
    left_columns.from_plus(0)
    right_rows_gather.z_far()
    right_rows_gather.x_neighbours(1)
    right_rows_gather.x_neighbours(2)
    left_columns.from_minus(1)
    left_columns.from_plus(1)
    left_columns.finish(0)
    left_columns.finish(1)
    right_rows_gather.x_neighbours(3)
    left_columns.finish_twin()

    for h in range(2):
        for g in range(6):
            left_t[128 * g : 128 * g + 128, 256 * h : 256 * h + 256] = left_all[8 * h + g].T
    for e in range(4):
        right_rows_gather.x_far(e)

    counts = sum(
        dot(left_all[8 * h + 6].T, right_all[h, :, 768:896]) for h in range(2)
    )
    counts = jnp.maximum(counts[:24], 1.0)
    for g in range(3):
        rhs = right_all[:, :, 256 * g : 256 * g + 256].reshape(512, 256)
        outer = dot(left_t[...], rhs)
        for u in range(2):
            for c in range(32):
                lhs2[24 * (2 * g + u) : 24 * (2 * g + u) + 24, 128 * c : 128 * c + 128] = outer[
                    24 * c : 24 * c + 24, 128 * u : 128 * u + 128
                ]
    proj[...] = jnp.zeros((144, 512), F32)

    def project(t, carry):
        part = pl.ds(pl.multiple_of(t * 512, 512), 512)
        proj[...] += dot(lhs2[:, part].astype(BF16), bd[part, :])
        return carry

    lax.fori_loop(0, 8, project, 0)
    for g in range(6):
        for u in range(0, 4, 2):
            tiles = []
            for v in (u, u + 1):
                j = 4 * g + v
                tile = pairf[pl.ds(j, 24, stride=24), :] + proj[
                    24 * g : 24 * g + 24, 128 * v : 128 * v + 128
                ] / counts[:, j : j + 1]
                tiles.append(tile)
            rounded = jnp.concatenate(tiles, axis=0).astype(BF16).astype(F32)
            rows = slice(24 * (4 * g + u), 24 * (4 * g + u) + 48)
            first[rows, :] = rounded
            normed[rows, :] = norm(rounded).astype(BF16)

    def operands(t, carry):
        rows = pl.ds(pl.multiple_of(t * 96, 96), 96)
        p = dot(normed[rows, :], tproj_ref[...])
        m = pmask[rows, :]
        tri_left[q, rows, :] = (jax.nn.sigmoid(p[:, :128]) * p[:, 128:256] * m).astype(BF16)
        tri_send[rows, :] = (jax.nn.sigmoid(p[:, 256:384]) * p[:, 384:] * m).astype(BF16)
        return carry

    lax.fori_loop(0, 6, operands, 0)

    tri_columns = Columns(tri_left, 288, TRI_LEFT)
    tri_rows = Rows(
        lambda zz, xx: tri_right.at[xx, zz],
        lambda zz, xx, h: tri_right.at[xx, zz, pl.ds(2 * h, 2)],
        TRI_RIGHT,
    )
    holder, place = lax.rem(q, 4), q // 4

    def tri_scatter(t, carry):
        is_self = same & (t == z)
        piece = pl.ds(pl.multiple_of(t * 144, 144), 144)

        @pl.when(jnp.logical_not(is_self))
        def _():
            remote(
                tri_send.at[piece], tri_right.at[holder, t, place], TRI_SCATTER + t,
                TRI_SCATTER + place, (t * 4 + holder, r),
            ).start()

        @pl.when(is_self)
        def _():
            tri_right[holder, t, place] = tri_send[piece, :]

        return carry

    lax.fori_loop(0, 4, tri_scatter, 0)
    tri_columns.start()

    def tri_arrived(t, carry):
        @pl.when(jnp.logical_not(same & (t == place)))
        def _():
            piece = tri_right.at[x, z, t]
            remote(piece, piece, TRI_SCATTER + t, TRI_SCATTER + t, twin).wait_recv()

        return carry

    lax.fori_loop(0, 4, tri_arrived, 0)
    tri_rows.start()
    tri_columns.other_half()

    def gates(t, carry):
        rows = pl.ds(pl.multiple_of(t * 96, 96), 96)
        gate[rows, :] = jax.nn.sigmoid(dot(normed[rows, :], tgate_ref[...]))
        summed[rows, :] = jnp.zeros((96, 128), F32)
        return carry

    lax.fori_loop(0, 6, gates, 0)

    def accumulate(xx, zz):
        def widen(t, carry):
            rf[pl.ds(pl.multiple_of(t * 144, 144), 144), :] = tri_right[xx, zz, t].astype(F32)
            return carry

        lax.fori_loop(0, 4, widen, 0)
        for half in range(2):
            base = half * 12

            def step(t, acc):
                b, kk = t // 3, lax.rem(t, 3)
                rows = pl.ds(pl.multiple_of(zz * 144 + kk * 48, 16), 48)
                two = tri_left[b * 4 + xx, rows, :].astype(F32)
                acc = list(acc)
                for v in range(2):
                    left = two[24 * v : 24 * v + 24]
                    for j in range(12):
                        row = rf[pl.ds(t * 48 + v * 24 + base + j, 1), :]
                        acc[j] = acc[j] + left * row
                return tuple(acc)

            acc = tuple(summed[24 * (base + j) : 24 * (base + j) + 24, :] for j in range(12))
            acc = lax.fori_loop(0, 12, step, acc)
            for j in range(12):
                summed[24 * (base + j) : 24 * (base + j) + 24, :] = acc[j]

    def xat(d):
        return lax.rem(x + d + 4, 4)

    tri_rows.z_neighbours()
    tri_columns.from_minus(0)
    tri_columns.from_plus(0)
    tri_rows.x_neighbours(0)
    tri_rows.z_far()
    tri_columns.from_minus(1)
    tri_columns.from_plus(1)
    tri_columns.finish(0)
    tri_columns.finish(1)
    tri_rows.x_neighbours(1)
    tri_columns.finish_twin()
    order = tri_rows.order
    accumulate(x, order[0])
    accumulate(x, order[1])
    tri_rows.x_neighbours(2)
    accumulate(x, order[2])
    accumulate(x, order[3])
    accumulate(xat(-1), order[0])
    accumulate(xat(1), order[0])
    tri_rows.x_neighbours(3)
    accumulate(xat(-1), order[1])
    accumulate(xat(1), order[1])
    accumulate(xat(-1), order[2])
    accumulate(xat(1), order[2])
    accumulate(xat(-1), order[3])
    accumulate(xat(1), order[3])
    for e in range(4):
        tri_rows.x_far(e)
        accumulate(xat(2), order[e])

    def finish(t, carry):
        rows = pl.ds(pl.multiple_of(t * 96, 96), 96)
        normed_sum = norm(summed[rows, :]).astype(BF16)
        second = (first[rows, :] + gate[rows, :] * dot(normed_sum, tout_ref[...])).astype(BF16)
        second = second.astype(F32)
        hidden = jnp.maximum(dot(norm(second).astype(BF16), tin_ref[...]), 0.0).astype(BF16)
        pairf[rows, :] = second + dot(hidden, trans_ref[...])
        return carry

    lax.fori_loop(0, 6, finish, 0)
    for i in range(0, 24, 2):
        out_ref[24 * i : 24 * i + 48, :] = jnp.concatenate(
            [pairf[pl.ds(i + v, 24, stride=24), :] for v in range(2)], axis=0
        ).astype(BF16)

    def scatter_left(t, carry):
        @pl.when(jnp.logical_not(same & (t == q)))
        def _():
            remote(
                left_send.at[t], left_send.at[t], LEFT_SCATTER + t, LEFT_SCATTER + t, twin
            ).wait_send()

        return carry

    lax.fori_loop(0, 16, scatter_left, 0)

    def tri_left_here(t, carry):
        @pl.when(jnp.logical_not(same & (t == z)))
        def _():
            piece = tri_send.at[pl.ds(pl.multiple_of(t * 144, 144), 144)]
            remote(piece, piece, TRI_SCATTER + t, TRI_SCATTER + t, twin).wait_send()

        return carry

    lax.fori_loop(0, 4, tri_left_here, 0)
    left_columns.drain()
    right_rows_gather.drain()
    tri_columns.drain()
    tri_rows.drain()


def shards(alignment, alignment_mask, residue_mask, pair_features, *weights):
    vmem = pl.BlockSpec(memory_space=pltpu.VMEM)
    smem = pl.BlockSpec(memory_space=pltpu.SMEM)
    out = pl.pallas_call(
        kernel,
        out_shape=jax.ShapeDtypeStruct((576, 128), BF16),
        in_specs=[vmem, vmem, smem] + [vmem] * 9,
        out_specs=vmem,
        scratch_shapes=[
            pltpu.VMEM((2, 768, 128), F32),
            pltpu.VMEM((1024, 256), BF16),
            pltpu.VMEM((768, 768), BF16),
            pltpu.VMEM((4096, 512), BF16),
            pltpu.VMEM((32, 768), BF16),
            pltpu.VMEM((16, 16, 128), BF16),
            pltpu.VMEM((16, 256, 128), BF16),
            pltpu.VMEM((2, 256, 896), BF16),
            pltpu.VMEM((768, 512), BF16),
            pltpu.VMEM((144, 4096), F32),
            pltpu.VMEM((576, 128), F32),
            pltpu.VMEM((576, 128), F32),
            pltpu.VMEM((576, 128), BF16),
            pltpu.VMEM((576, 128), F32),
            pltpu.VMEM((144, 512), F32),
            pltpu.VMEM((576, 128), F32),
            pltpu.VMEM((16, 576, 128), BF16),
            pltpu.VMEM((576, 128), BF16),
            pltpu.VMEM((4, 4, 4, 144, 128), BF16),
            pltpu.VMEM((576, 128), F32),
            pltpu.VMEM((576, 128), F32),
            pltpu.SemaphoreType.DMA((TRANSFERS,)),
            pltpu.SemaphoreType.DMA((TRANSFERS,)),
        ],
        compiler_params=pltpu.CompilerParams(
            collective_id=0, has_side_effects=True, vmem_limit_bytes=48 * 1024 * 1024
        ),
        cost_estimate=pl.CostEstimate(
            flops=1_500_000_000, bytes_accessed=2_000_000, transcendentals=400_000
        ),
    )(
        alignment.reshape(768, 256), alignment_mask, residue_mask, pair_features.reshape(576, 128),
        *weights,
    )
    return out.reshape(24, 24, 128)


def solution(mesh):
    placed = (P("row", "col", None), P("row", "col"), P(), P("row", "col", None)) + (P(),) * 8
    return jax.shard_map(
        shards, mesh=mesh, in_specs=placed, out_specs=P("row", "col", None), check_vma=False
    )
```

```python
import jax
import jax.numpy as jnp
from jax import lax
from jax.experimental import pallas as pl
from jax.experimental.pallas import tpu as pltpu
from jax.sharding import PartitionSpec as P

EPSILON = 1e-05
MESH = pl.DeviceIdType.MESH
F32 = jnp.float32
BF16 = jnp.bfloat16
I32 = jnp.int32

LEFT_SCATTER = 0
LEFT_GATHER = 16
RIGHT_GATHER = 33
TRI_SCATTER = 53
TRI_LEFT = 57
TRI_RIGHT = 74
TRANSFERS = 94


def norm(v):
    mean = jnp.mean(v, axis=-1, keepdims=True)
    centered = v - mean
    variance = jnp.mean(centered * centered, axis=-1, keepdims=True)
    return centered * lax.rsqrt(variance + EPSILON)


def dot(a, b):
    return jnp.dot(a, b, preferred_element_type=F32)


def kernel(
    align_hbm, amask_hbm, rmask_hbm, pair_hbm, wl_hbm, wr_hbm, oproj_hbm, tproj_hbm, tgate_hbm,
    tout_hbm, tin_hbm, trans_hbm, out_ref,
    align_ref, amask_ref, rmask_ref, pair_ref, wl_ref, wr_ref, oproj_ref, tproj_ref, tgate_ref,
    tout_ref, tin_ref, trans_ref,
    xs, wbd, perm, bd, lnat, left_send, left_all, right_all, left_t, lhs2, ptile, first, normed,
    pmask, gate, tri_left, tri_send, tri_right, lf, rf, part, ss, rs, ls,
):
    loads = {
        name: pltpu.make_async_copy(src, dst, ls.at[n])
        for n, (name, src, dst) in enumerate(
            (
                ("align", align_hbm, align_ref),
                ("wl", wl_hbm, wl_ref),
                ("wr", wr_hbm, wr_ref),
                ("amask", amask_hbm, amask_ref),
                ("oproj", oproj_hbm, oproj_ref),
                ("rmask", rmask_hbm, rmask_ref),
                ("pair", pair_hbm, pair_ref),
                ("tproj", tproj_hbm, tproj_ref),
                ("tgate", tgate_hbm, tgate_ref),
                ("tout", tout_hbm, tout_ref),
                ("tin", tin_hbm, tin_ref),
                ("trans", trans_hbm, trans_ref),
            )
        )
    }
    r, q = lax.axis_index("row"), lax.axis_index("col")
    z, x = r // 4, lax.rem(r, 4)
    zl, y, core = q // 8, lax.rem(q // 2, 4), lax.rem(q, 2)
    same = r == q

    def row_of(zz, xx):
        return lax.rem(zz + 4, 4) * 4 + lax.rem(xx + 4, 4)

    def col_of(ll, yy, cc):
        return (ll * 4 + lax.rem(yy + 4, 4)) * 2 + cc

    zp, zm = (row_of(z + 1, x), q), (row_of(z - 1, x), q)
    xp, xm = (row_of(z, x + 1), q), (row_of(z, x - 1), q)
    yp, ym = (r, col_of(zl, y + 1, core)), (r, col_of(zl, y - 1, core))
    zlo = (r, col_of(1 - zl, y, core))
    twin = (r, col_of(zl, y, 1 - core))

    barrier = pltpu.get_barrier_semaphore()
    for device in (zp, zm, xp, xm, yp, ym, zlo, twin):
        pl.semaphore_signal(barrier, inc=1, device_id=device, device_id_type=MESH)

    def greet(t, carry):
        @pl.when(jnp.logical_not(same & (t == r)))
        def _():
            pl.semaphore_signal(barrier, inc=1, device_id=(t, r), device_id_type=MESH)

        return carry

    lax.fori_loop(0, 16, greet, 0)

    def greet_tri(t, carry):
        @pl.when(jnp.logical_not(same & (t * 4 + x == q)))
        def _():
            pl.semaphore_signal(barrier, inc=1, device_id=(q, t * 4 + x), device_id_type=MESH)

        return carry

    lax.fori_loop(0, 4, greet_tri, 0)

    for load in loads.values():
        load.start()

    loads["align"].wait()

    def norm_chunk(t, carry):
        rows = pl.ds(pl.multiple_of(t * 96, 96), 96)
        v = norm(align_ref[rows, :].astype(F32))
        xs[0, rows, :] = v[:, :128]
        xs[1, rows, :] = v[:, 128:]
        return carry

    lax.fori_loop(0, 8, norm_chunk, 0)

    lane = lax.broadcasted_iota(I32, (256, 128), 1)
    spread = (
        lax.rem(lax.broadcasted_iota(I32, (32, 128), 1), 32)
        == lax.broadcasted_iota(I32, (32, 128), 0)
    ).astype(F32).astype(BF16)
    loads["wl"].wait()
    loads["wr"].wait()
    for side, w_ref in enumerate((wl_ref, wr_ref)):
        w = dot(w_ref[...].astype(F32).T.astype(BF16), spread)
        for u in range(4):
            own = (lane >= 32 * u) & (lane < 32 * u + 32)
            wbd[256 * u : 256 * u + 256, 128 * side : 128 * side + 128] = jnp.where(
                own, w, 0.0
            ).astype(BF16)

    lam = lax.broadcasted_iota(I32, (1, 768), 1)
    by24 = (lam * 2731) // 65536
    target = (lam - by24 * 24) * 32 + by24

    def perm_chunk(t, carry):
        start = pl.multiple_of(t * 64, 64)
        rows = lax.broadcasted_iota(I32, (64, 768), 0) + start
        perm[pl.ds(start, 64), :] = (rows == target).astype(F32).astype(BF16)
        return carry

    lax.fori_loop(0, 12, perm_chunk, 0)

    loads["amask"].wait()
    amask = amask_ref[...].astype(F32).T.astype(BF16)
    row24 = lax.broadcasted_iota(I32, (24, 768), 0) * 32
    lane24 = lax.broadcasted_iota(I32, (24, 768), 1)
    expand = ((lane24 >= row24) & (lane24 < row24 + 32)).astype(F32).astype(BF16)
    mask_wide = dot(amask, expand)
    mask_lanes = dot(
        amask,
        (
            lax.broadcasted_iota(I32, (24, 128), 0) == lax.broadcasted_iota(I32, (24, 128), 1)
        ).astype(F32).astype(BF16),
    ).astype(BF16)
    for g in range(6):
        four = jnp.concatenate(
            [
                xs[half, pl.ds(4 * g + u, 32, stride=24), :].astype(BF16)
                for u in range(4)
                for half in range(2)
            ],
            axis=1,
        )
        both = dot(four, wbd[...])
        m = mask_wide[:, 128 * g : 128 * g + 128]
        lnat[:, 128 * g : 128 * g + 128] = (both[:, :128] * m).astype(BF16)
        right = (both[:, 128:] * m).astype(BF16)
        for h in range(2):
            right_all[h, pl.ds(pl.multiple_of(r * 16, 16), 16), 128 * g : 128 * g + 128] = right[
                16 * h : 16 * h + 16
            ]
    left = dot(lnat[...], perm[...]).astype(BF16)
    for h in range(2):
        right_all[h, pl.ds(pl.multiple_of(r * 16, 16), 16), 768:896] = mask_lanes[
            16 * h : 16 * h + 16
        ]
        for g in range(6):
            left_send[8 * h + g] = left[16 * h : 16 * h + 16, 128 * g : 128 * g + 128]
        left_send[8 * h + 6] = mask_lanes[16 * h : 16 * h + 16]
        left_send[8 * h + 7] = jnp.zeros((16, 128), BF16)

    def remote(src, dst, send, recv, device):
        return pltpu.make_async_remote_copy(
            src_ref=src, dst_ref=dst, send_sem=ss.at[send], recv_sem=rs.at[recv],
            device_id=device, device_id_type=MESH,
        )

    def send(ref, k, device):
        remote(ref, ref, k, k, device).start()

    def wait_recv(ref, k):
        remote(ref, ref, k, k, twin).wait_recv()

    def wait_send(ref, k):
        remote(ref, ref, k, k, twin).wait_send()

    class Ring:
        def __init__(self, slot, half, at, plus, minus, k):
            self.slot, self.half, self.at = slot, half, at
            self.plus, self.minus, self.k = plus, minus, k

        def pos(self, d):
            return lax.rem(self.at + d + 4, 4)

        def start(self):
            send(self.slot(self.at), self.k, self.plus)
            send(self.slot(self.at), self.k + 1, self.minus)

        def from_minus(self):
            wait_recv(self.slot(self.pos(-1)), self.k)
            send(self.half(self.pos(-1), 0), self.k + 2, self.plus)

        def from_plus(self):
            wait_recv(self.slot(self.pos(1)), self.k + 1)
            send(self.half(self.pos(1), 1), self.k + 3, self.minus)

        def finish(self):
            wait_recv(self.half(self.pos(2), 0), self.k + 2)
            wait_recv(self.half(self.pos(2), 1), self.k + 3)

        def drain(self):
            wait_send(self.slot(self.at), self.k)
            wait_send(self.slot(self.at), self.k + 1)
            wait_send(self.half(self.pos(-1), 0), self.k + 2)
            wait_send(self.half(self.pos(1), 1), self.k + 3)

    class Columns:
        def __init__(self, ref, half_rows, k):
            self.ref, self.k = ref, k

            def slot(ll):
                return lambda yy: ref.at[col_of(ll, yy, core)]

            def half(ll):
                return lambda yy, h: ref.at[
                    col_of(ll, yy, core), pl.ds(h * half_rows, half_rows)
                ]

            self.rings = [
                Ring(slot(ll), half(ll), y, yp, ym, k + 1 + 4 * e)
                for e, ll in enumerate((zl, 1 - zl))
            ]
            self.passed = []

        def to_twin(self, ll, yy):
            n = len(self.passed)
            at = lax.rem(yy + 4, 4)
            self.passed.append((ll, at))
            send(self.ref.at[col_of(ll, at, core)], self.k + 9 + n, twin)

        def start(self):
            send(self.ref.at[q], self.k, zlo)
            self.rings[0].start()
            self.to_twin(zl, y)

        def other_half(self):
            wait_recv(self.ref.at[col_of(1 - zl, y, core)], self.k)
            self.rings[1].start()
            self.to_twin(1 - zl, y)

        def from_minus(self, e):
            self.rings[e].from_minus()
            self.to_twin((zl, 1 - zl)[e], y - 1)

        def from_plus(self, e):
            self.rings[e].from_plus()
            self.to_twin((zl, 1 - zl)[e], y + 1)

        def finish(self, e):
            self.rings[e].finish()
            self.to_twin((zl, 1 - zl)[e], y + 2)

        def finish_twin(self):
            for n, (ll, at) in enumerate(self.passed):
                wait_recv(self.ref.at[col_of(ll, at, 1 - core)], self.k + 9 + n)

        def drain(self):
            wait_send(self.ref.at[q], self.k)
            for ring in self.rings:
                ring.drain()
            for n, (ll, at) in enumerate(self.passed):
                wait_send(self.ref.at[col_of(ll, at, core)], self.k + 9 + n)

    class Rows:
        def __init__(self, block, half, k):
            self.zring = Ring(
                lambda zz: block(zz, x), lambda zz, h: half(zz, x, h), z, zp, zm, k
            )

            def slot(zz):
                return lambda xx: block(zz, xx)

            def part(zz):
                return lambda xx, h: half(zz, xx, h)

            self.order = [z, lax.rem(z + 3, 4), lax.rem(z + 1, 4), lax.rem(z + 2, 4)]
            self.xrings = [
                Ring(slot(zz), part(zz), x, xp, xm, k + 4 + 4 * e)
                for e, zz in enumerate(self.order)
            ]

        def start(self):
            self.zring.start()
            self.xrings[0].start()

        def z_neighbours(self):
            self.zring.from_minus()
            self.xrings[1].start()
            self.zring.from_plus()
            self.xrings[2].start()

        def z_far(self):
            self.zring.finish()
            self.xrings[3].start()

        def x_neighbours(self, e):
            self.xrings[e].from_minus()
            self.xrings[e].from_plus()

        def x_far(self, e):
            self.xrings[e].finish()

        def drain(self):
            self.zring.drain()
            for ring in self.xrings:
                ring.drain()

    def right_rows(zz, xx):
        return pl.ds(pl.multiple_of((zz * 4 + xx) * 16, 16), 16)

    right_rows_gather = Rows(
        lambda zz, xx: right_all.at[:, right_rows(zz, xx), :],
        lambda zz, xx, h: right_all.at[pl.ds(h, 1), right_rows(zz, xx), :],
        RIGHT_GATHER,
    )
    left_columns = Columns(left_all, 128, LEFT_GATHER)

    def zero_chunk(t, carry):
        bd[pl.ds(pl.multiple_of(t * 128, 128), 128), :] = jnp.zeros((128, 512), BF16)
        part[pl.ds(pl.multiple_of(t * 144, 144), 144), :] = jnp.zeros((144, 128), F32)
        return carry

    lax.fori_loop(0, 32, zero_chunk, 0)
    loads["oproj"].wait()

    def fill_chunk(t, carry):
        block = oproj_ref[pl.ds(pl.multiple_of(t * 32, 32), 32), :]
        for u in range(4):
            bd[pl.ds(pl.multiple_of(t * 128 + 32 * u, 32), 32), 128 * u : 128 * u + 128] = block
        return carry

    lax.fori_loop(0, 32, fill_chunk, 0)
    loads["rmask"].wait()
    mask_k = jnp.zeros((24, 128), F32)
    sub = lax.broadcasted_iota(I32, (24, 128), 0)
    for k in range(24):
        mask_k = jnp.where(sub == k, rmask_ref[q * 24 + k].astype(F32), mask_k)
    for i in range(24):
        pmask[24 * i : 24 * i + 24, :] = mask_k * rmask_ref[r * 24 + i].astype(F32)
    for name in ("pair", "tproj", "tgate", "tout", "tin", "trans"):
        loads[name].wait()

    pl.semaphore_wait(barrier, 28 - 2 * same.astype(I32))

    right_rows_gather.start()
    own_rows = pl.ds(pl.multiple_of(r * 16, 16), 16)

    def scatter(t, carry):
        is_self = same & (t == q)

        @pl.when(jnp.logical_not(is_self))
        def _():
            remote(
                left_send.at[t], left_all.at[t, own_rows], LEFT_SCATTER + t, LEFT_SCATTER + r, (q, t)
            ).start()

        @pl.when(is_self)
        def _():
            left_all[t, own_rows] = left_send[t]

        return carry

    lax.fori_loop(0, 16, scatter, 0)

    def scatter_arrived(t, carry):
        @pl.when(jnp.logical_not(same & (t == r)))
        def _():
            piece = left_all.at[q, pl.ds(pl.multiple_of(t * 16, 16), 16)]
            remote(piece, piece, LEFT_SCATTER + t, LEFT_SCATTER + t, twin).wait_recv()

        return carry

    lax.fori_loop(0, 16, scatter_arrived, 0)
    left_columns.start()
    right_rows_gather.z_neighbours()
    left_columns.other_half()

    right_rows_gather.x_neighbours(0)
    left_columns.from_minus(0)
    left_columns.from_plus(0)
    right_rows_gather.z_far()
    right_rows_gather.x_neighbours(1)
    right_rows_gather.x_neighbours(2)
    left_columns.from_minus(1)
    left_columns.from_plus(1)
    left_columns.finish(0)
    left_columns.finish(1)
    right_rows_gather.x_neighbours(3)
    left_columns.finish_twin()

    for h in range(2):
        for g in range(6):
            left_t[128 * g : 128 * g + 128, 256 * h : 256 * h + 256] = left_all[8 * h + g].T
    for e in range(4):
        right_rows_gather.x_far(e)

    counts = sum(
        dot(left_all[8 * h + 6].T, right_all[h, :, 768:896]) for h in range(2)
    )
    counts = jnp.maximum(counts[:24], 1.0)
    for g in range(3):
        rhs = right_all[:, :, 256 * g : 256 * g + 256].reshape(512, 256)
        outer = dot(left_t[...], rhs)
        for u in range(2):
            for c in range(32):
                lhs2[32 * (2 * g + u) : 32 * (2 * g + u) + 24, 128 * c : 128 * c + 128] = outer[
                    24 * c : 24 * c + 24, 128 * u : 128 * u + 128
                ].astype(BF16)
    for n in range(2):
        proj = dot(lhs2[...], bd[:, 256 * n : 256 * n + 256])
        for g in range(6):
            for u in range(2):
                j = 4 * g + 2 * n + u
                ptile[24 * j : 24 * j + 24, :] = (
                    proj[32 * g : 32 * g + 24, 128 * u : 128 * u + 128] / counts[:, j : j + 1]
                )
    for i in range(0, 24, 2):
        rows = slice(24 * i, 24 * i + 48)
        tiles = [ptile[pl.ds(i + v, 24, stride=24), :] for v in range(2)]
        rounded = (pair_ref[rows, :].astype(F32) + jnp.concatenate(tiles, axis=0)).astype(BF16)
        rounded = rounded.astype(F32)
        first[rows, :] = rounded
        normed[rows, :] = norm(rounded).astype(BF16)

    for t in range(3):
        rows = slice(192 * t, 192 * t + 192)
        p = dot(normed[rows, :], tproj_ref[...])
        m = pmask[rows, :]
        tri_left[q, rows, :] = (jax.nn.sigmoid(p[:, :128]) * p[:, 128:256] * m).astype(BF16)
        tri_send[rows, :] = (jax.nn.sigmoid(p[:, 256:384]) * p[:, 384:] * m).astype(BF16)

    tri_columns = Columns(tri_left, 288, TRI_LEFT)
    tri_rows = Rows(
        lambda zz, xx: tri_right.at[xx, zz],
        lambda zz, xx, h: tri_right.at[xx, zz, pl.ds(2 * h, 2)],
        TRI_RIGHT,
    )
    holder, place = lax.rem(q, 4), q // 4

    def tri_scatter(t, carry):
        is_self = same & (t == z)
        piece = pl.ds(pl.multiple_of(t * 144, 144), 144)

        @pl.when(jnp.logical_not(is_self))
        def _():
            remote(
                tri_send.at[piece], tri_right.at[holder, t, place], TRI_SCATTER + t,
                TRI_SCATTER + place, (t * 4 + holder, r),
            ).start()

        @pl.when(is_self)
        def _():
            tri_right[holder, t, place] = tri_send[piece, :]

        return carry

    lax.fori_loop(0, 4, tri_scatter, 0)
    tri_columns.start()

    def tri_arrived(t, carry):
        @pl.when(jnp.logical_not(same & (t == place)))
        def _():
            piece = tri_right.at[x, z, t]
            remote(piece, piece, TRI_SCATTER + t, TRI_SCATTER + t, twin).wait_recv()

        return carry

    lax.fori_loop(0, 4, tri_arrived, 0)
    tri_rows.start()
    tri_columns.other_half()

    gate[...] = jax.nn.sigmoid(dot(normed[...], tgate_ref[...]))

    def widen_left(xx):
        def widen(t, carry):
            b, rows = t // 4, pl.ds(pl.multiple_of(lax.rem(t, 4) * 144, 144), 144)
            lf[xx, b, rows, :] = tri_left[b * 4 + xx, rows, :].astype(F32)
            return carry

        lax.fori_loop(0, 16, widen, 0)

    def accumulate(xx, zz):
        def widen(t, carry):
            rf[t] = tri_right[xx, zz, t].astype(F32)
            return carry

        lax.fori_loop(0, 4, widen, 0)

        def block(t, carry):
            def at(u, v):
                return pl.ds(pl.multiple_of(((t * 4 + u) * 24 + zz * 6 + v) * 8, 8), 8)

            acc = [[part[at(u, v), :] for v in range(6)] for u in range(4)]
            for b in range(4):
                for k in range(3):
                    left = [
                        lf[xx, b, pl.ds(pl.multiple_of((t * 4 + u) * 24 + 8 * k, 8), 8), :]
                        for u in range(4)
                    ]
                    right = [rf[b, 24 * v + 8 * k : 24 * v + 8 * k + 8, :] for v in range(6)]
                    for u in range(4):
                        for v in range(6):
                            acc[u][v] = acc[u][v] + left[u] * right[v]
            for u in range(4):
                for v in range(6):
                    part[at(u, v), :] = acc[u][v]
            return carry

        lax.fori_loop(0, 6, block, 0)

    def xat(d):
        return lax.rem(x + d + 4, 4)

    tri_rows.z_neighbours()
    tri_columns.from_minus(0)
    tri_columns.from_plus(0)
    tri_rows.x_neighbours(0)
    tri_rows.z_far()
    tri_columns.from_minus(1)
    tri_columns.from_plus(1)
    tri_columns.finish(0)
    tri_columns.finish(1)
    tri_rows.x_neighbours(1)
    tri_columns.finish_twin()
    order = tri_rows.order
    widen_left(x)
    accumulate(x, order[0])
    accumulate(x, order[1])
    tri_rows.x_neighbours(2)
    accumulate(x, order[2])
    accumulate(x, order[3])
    widen_left(xat(-1))
    widen_left(xat(1))
    accumulate(xat(-1), order[0])
    accumulate(xat(1), order[0])
    tri_rows.x_neighbours(3)
    accumulate(xat(-1), order[1])
    accumulate(xat(1), order[1])
    accumulate(xat(-1), order[2])
    accumulate(xat(1), order[2])
    accumulate(xat(-1), order[3])
    accumulate(xat(1), order[3])
    widen_left(xat(2))
    for e in range(4):
        tri_rows.x_far(e)
        accumulate(xat(2), order[e])

    for t in range(2):
        rows = slice(288 * t, 288 * t + 288)
        summed = part[pl.ds(2304 * t, 288, stride=8), :]
        for k in range(1, 8):
            summed = summed + part[pl.ds(2304 * t + k, 288, stride=8), :]
        normed_sum = norm(summed).astype(BF16)
        second = (first[rows, :] + gate[rows, :] * dot(normed_sum, tout_ref[...])).astype(BF16)
        second = second.astype(F32)
        hidden = jnp.maximum(dot(norm(second).astype(BF16), tin_ref[...]), 0.0).astype(BF16)
        out_ref[rows, :] = (second + dot(hidden, trans_ref[...])).astype(BF16)

    def scatter_left(t, carry):
        @pl.when(jnp.logical_not(same & (t == q)))
        def _():
            remote(
                left_send.at[t], left_send.at[t], LEFT_SCATTER + t, LEFT_SCATTER + t, twin
            ).wait_send()

        return carry

    lax.fori_loop(0, 16, scatter_left, 0)

    def tri_left_here(t, carry):
        @pl.when(jnp.logical_not(same & (t == z)))
        def _():
            piece = tri_send.at[pl.ds(pl.multiple_of(t * 144, 144), 144)]
            remote(piece, piece, TRI_SCATTER + t, TRI_SCATTER + t, twin).wait_send()

        return carry

    lax.fori_loop(0, 4, tri_left_here, 0)
    left_columns.drain()
    right_rows_gather.drain()
    tri_columns.drain()
    tri_rows.drain()


def shards(alignment, alignment_mask, residue_mask, pair_features, *weights):
    vmem = pl.BlockSpec(memory_space=pltpu.VMEM)
    hbm = pl.BlockSpec(memory_space=pltpu.HBM)
    out = pl.pallas_call(
        kernel,
        out_shape=jax.ShapeDtypeStruct((576, 128), BF16),
        in_specs=[hbm] * 12,
        out_specs=vmem,
        scratch_shapes=[
            pltpu.VMEM((768, 256), BF16),
            pltpu.VMEM((24, 32), I32),
            pltpu.SMEM((384,), I32),
            pltpu.VMEM((576, 128), BF16),
            pltpu.VMEM((32, 256), BF16),
            pltpu.VMEM((32, 256), BF16),
            pltpu.VMEM((1024, 128), BF16),
            pltpu.VMEM((128, 512), BF16),
            pltpu.VMEM((128, 128), BF16),
            pltpu.VMEM((128, 128), BF16),
            pltpu.VMEM((128, 512), BF16),
            pltpu.VMEM((512, 128), BF16),
            pltpu.VMEM((2, 768, 128), F32),
            pltpu.VMEM((1024, 256), BF16),
            pltpu.VMEM((768, 768), BF16),
            pltpu.VMEM((4096, 512), BF16),
            pltpu.VMEM((32, 768), BF16),
            pltpu.VMEM((16, 16, 128), BF16),
            pltpu.VMEM((16, 256, 128), BF16),
            pltpu.VMEM((2, 256, 896), BF16),
            pltpu.VMEM((768, 512), BF16),
            pltpu.VMEM((192, 4096), BF16),
            pltpu.VMEM((576, 128), F32),
            pltpu.VMEM((576, 128), F32),
            pltpu.VMEM((576, 128), BF16),
            pltpu.VMEM((576, 128), F32),
            pltpu.VMEM((576, 128), F32),
            pltpu.VMEM((16, 576, 128), BF16),
            pltpu.VMEM((576, 128), BF16),
            pltpu.VMEM((4, 4, 4, 144, 128), BF16),
            pltpu.VMEM((4, 4, 576, 128), F32),
            pltpu.VMEM((4, 144, 128), F32),
            pltpu.VMEM((4608, 128), F32),
            pltpu.SemaphoreType.DMA((TRANSFERS,)),
            pltpu.SemaphoreType.DMA((TRANSFERS,)),
            pltpu.SemaphoreType.DMA((12,)),
        ],
        compiler_params=pltpu.CompilerParams(
            collective_id=0, has_side_effects=True, vmem_limit_bytes=60 * 1024 * 1024
        ),
        cost_estimate=pl.CostEstimate(
            flops=1_500_000_000, bytes_accessed=2_000_000, transcendentals=400_000
        ),
    )(
        alignment.reshape(768, 256), alignment_mask.T, residue_mask, pair_features.reshape(576, 128),
        weights[0].T, weights[1].T, *weights[2:],
    )
    return out.reshape(24, 24, 128)


def solution(mesh):
    placed = (P("row", "col", None), P("row", "col"), P(), P("row", "col", None)) + (P(),) * 8
    return jax.shard_map(
        shards, mesh=mesh, in_specs=placed, out_specs=P("row", "col", None), check_vma=False
    )
```

```python
import jax
import jax.numpy as jnp
from jax import lax
from jax.experimental import pallas as pl
from jax.experimental.pallas import tpu as pltpu
from jax.sharding import PartitionSpec as P

EPSILON = 1e-05
MESH = pl.DeviceIdType.MESH
F32 = jnp.float32
BF16 = jnp.bfloat16
I32 = jnp.int32

LEFT_SCATTER = 0
LEFT_GATHER = 4
RIGHT_GATHER = 21
TRI_SCATTER = 41
TRI_LEFT = 45
TRI_RIGHT = 62
TRANSFERS = 102


def norm(v):
    mean = jnp.mean(v, axis=-1, keepdims=True)
    centered = v - mean
    variance = jnp.mean(centered * centered, axis=-1, keepdims=True)
    return centered * lax.rsqrt(variance + EPSILON)


def dot(a, b):
    return jnp.dot(a, b, preferred_element_type=F32)


def kernel(
    align_hbm, amask_hbm, rmask_hbm, pair_hbm, wl_hbm, wr_hbm, oproj_hbm, tproj_hbm, tgate_hbm,
    tout_hbm, tin_hbm, trans_hbm, out_ref,
    align_ref, amask_ref, rmask_ref, pair_ref, wl_ref, wr_ref, oproj_ref, tproj_ref, tgate_ref,
    tout_ref, tin_ref, trans_ref,
    xs, wbd, perm, bd, lnat, left_send, left_all, right_all, left_t, lhs2, ptile, first, normed,
    pmask, gate, tri_left, tri_send, tri_right, lf, rf, part, ss, rs, ls,
):
    loads = {
        name: pltpu.make_async_copy(src, dst, ls.at[n])
        for n, (name, src, dst) in enumerate(
            (
                ("align", align_hbm, align_ref),
                ("wl", wl_hbm, wl_ref),
                ("wr", wr_hbm, wr_ref),
                ("amask", amask_hbm, amask_ref),
                ("oproj", oproj_hbm, oproj_ref),
                ("rmask", rmask_hbm, rmask_ref),
                ("pair", pair_hbm, pair_ref),
                ("tproj", tproj_hbm, tproj_ref),
                ("tgate", tgate_hbm, tgate_ref),
                ("tout", tout_hbm, tout_ref),
                ("tin", tin_hbm, tin_ref),
                ("trans", trans_hbm, trans_ref),
            )
        )
    }
    r, q = lax.axis_index("row"), lax.axis_index("col")
    z, x = r // 4, lax.rem(r, 4)
    zl, y, core = q // 8, lax.rem(q // 2, 4), lax.rem(q, 2)
    same = r == q

    def row_of(zz, xx):
        return lax.rem(zz + 4, 4) * 4 + lax.rem(xx + 4, 4)

    def col_of(ll, yy, cc):
        return (ll * 4 + lax.rem(yy + 4, 4)) * 2 + cc

    zp, zm = (row_of(z + 1, x), q), (row_of(z - 1, x), q)
    xp, xm = (row_of(z, x + 1), q), (row_of(z, x - 1), q)
    yp, ym = (r, col_of(zl, y + 1, core)), (r, col_of(zl, y - 1, core))
    zlo = (r, col_of(1 - zl, y, core))
    twin = (r, col_of(zl, y, 1 - core))
    dp, dm = (r, col_of(1 - zl, y + 1, core)), (r, col_of(1 - zl, y - 1, core))

    barrier = pltpu.get_barrier_semaphore()
    for device in (zp, zm, xp, xm, yp, ym, zlo, twin, dp, dm):
        pl.semaphore_signal(barrier, inc=1, device_id=device, device_id_type=MESH)

    def greet(t, carry):
        @pl.when(jnp.logical_not(same & (t == z)))
        def _():
            pl.semaphore_signal(
                barrier, inc=1, device_id=(t * 4 + lax.rem(q, 4), r), device_id_type=MESH
            )

        return carry

    lax.fori_loop(0, 4, greet, 0)

    def greet_tri(t, carry):
        @pl.when(jnp.logical_not(same & (t * 4 + x == q)))
        def _():
            pl.semaphore_signal(barrier, inc=1, device_id=(q, t * 4 + x), device_id_type=MESH)

        return carry

    lax.fori_loop(0, 4, greet_tri, 0)

    for load in loads.values():
        load.start()

    loads["align"].wait()

    def norm_chunk(t, carry):
        rows = pl.ds(pl.multiple_of(t * 96, 96), 96)
        v = norm(align_ref[rows, :].astype(F32))
        xs[0, rows, :] = v[:, :128]
        xs[1, rows, :] = v[:, 128:]
        return carry

    lax.fori_loop(0, 8, norm_chunk, 0)

    lane = lax.broadcasted_iota(I32, (256, 128), 1)
    spread = (
        lax.rem(lax.broadcasted_iota(I32, (32, 128), 1), 32)
        == lax.broadcasted_iota(I32, (32, 128), 0)
    ).astype(F32).astype(BF16)
    loads["wl"].wait()
    loads["wr"].wait()
    for side, w_ref in enumerate((wl_ref, wr_ref)):
        w = dot(w_ref[...].astype(F32).T.astype(BF16), spread)
        for u in range(4):
            own = (lane >= 32 * u) & (lane < 32 * u + 32)
            wbd[256 * u : 256 * u + 256, 128 * side : 128 * side + 128] = jnp.where(
                own, w, 0.0
            ).astype(BF16)

    lam = lax.broadcasted_iota(I32, (1, 768), 1)
    by24 = (lam * 2731) // 65536
    target = (lam - by24 * 24) * 32 + by24

    def perm_chunk(t, carry):
        start = pl.multiple_of(t * 64, 64)
        rows = lax.broadcasted_iota(I32, (64, 768), 0) + start
        perm[pl.ds(start, 64), :] = (rows == target).astype(F32).astype(BF16)
        return carry

    lax.fori_loop(0, 12, perm_chunk, 0)

    loads["amask"].wait()
    amask = amask_ref[...].astype(F32).T.astype(BF16)
    row24 = lax.broadcasted_iota(I32, (24, 768), 0) * 32
    lane24 = lax.broadcasted_iota(I32, (24, 768), 1)
    expand = ((lane24 >= row24) & (lane24 < row24 + 32)).astype(F32).astype(BF16)
    mask_wide = dot(amask, expand)
    mask_lanes = dot(
        amask,
        (
            lax.broadcasted_iota(I32, (24, 128), 0) == lax.broadcasted_iota(I32, (24, 128), 1)
        ).astype(F32).astype(BF16),
    ).astype(BF16)
    own_rows = pl.ds(pl.multiple_of((x * 4 + z) * 32, 32), 32)
    for g in range(6):
        four = jnp.concatenate(
            [
                xs[half, pl.ds(4 * g + u, 32, stride=24), :].astype(BF16)
                for u in range(4)
                for half in range(2)
            ],
            axis=1,
        )
        both = dot(four, wbd[...])
        m = mask_wide[:, 128 * g : 128 * g + 128]
        lnat[:, 128 * g : 128 * g + 128] = (both[:, :128] * m).astype(BF16)
        right = (both[:, 128:] * m).astype(BF16)
        right_all[own_rows, 128 * g : 128 * g + 128] = right
    left = dot(lnat[...], perm[...]).astype(BF16)
    right_all[own_rows, 768:896] = mask_lanes
    for g in range(6):
        left_send[g // 2, g % 2] = left[:, 128 * g : 128 * g + 128]
    left_send[3, 0] = mask_lanes
    left_send[3, 1] = jnp.zeros((32, 128), BF16)

    def remote(src, dst, send, recv, device):
        return pltpu.make_async_remote_copy(
            src_ref=src, dst_ref=dst, send_sem=ss.at[send], recv_sem=rs.at[recv],
            device_id=device, device_id_type=MESH,
        )

    def send(ref, k, device):
        remote(ref, ref, k, k, device).start()

    def wait_recv(ref, k):
        remote(ref, ref, k, k, twin).wait_recv()

    def wait_send(ref, k):
        remote(ref, ref, k, k, twin).wait_send()

    class Ring:
        def __init__(self, slot, half, at, plus, minus, k):
            self.slot, self.half, self.at = slot, half, at
            self.plus, self.minus, self.k = plus, minus, k

        def pos(self, d):
            return lax.rem(self.at + d + 4, 4)

        def start(self):
            send(self.slot(self.at), self.k, self.plus)
            send(self.slot(self.at), self.k + 1, self.minus)

        def from_minus(self):
            wait_recv(self.slot(self.pos(-1)), self.k)
            send(self.half(self.pos(-1), 0), self.k + 2, self.plus)

        def from_plus(self):
            wait_recv(self.slot(self.pos(1)), self.k + 1)
            send(self.half(self.pos(1), 1), self.k + 3, self.minus)

        def finish(self):
            wait_recv(self.half(self.pos(2), 0), self.k + 2)
            wait_recv(self.half(self.pos(2), 1), self.k + 3)

        def drain(self):
            wait_send(self.slot(self.at), self.k)
            wait_send(self.slot(self.at), self.k + 1)
            wait_send(self.half(self.pos(-1), 0), self.k + 2)
            wait_send(self.half(self.pos(1), 1), self.k + 3)

    class Columns:
        def __init__(self, ref, half_rows, k, diagonal):
            self.ref, self.k, self.diagonal = ref, k, diagonal

            def slot(ll):
                return lambda yy: ref.at[col_of(ll, yy, core)]

            def half(ll):
                return lambda yy, h: ref.at[
                    col_of(ll, yy, core), pl.ds(h * half_rows, half_rows)
                ]

            self.rings = [
                Ring(slot(ll), half(ll), y, yp, ym, k + 1 + 4 * e)
                for e, ll in enumerate((zl, 1 - zl))
            ]
            self.passed = []

        def to_twin(self, ll, yy):
            n = len(self.passed)
            at = lax.rem(yy + 4, 4)
            self.passed.append((ll, at))
            send(self.ref.at[col_of(ll, at, core)], self.k + 9 + n, twin)

        def start(self):
            send(self.ref.at[q], self.k, zlo)
            self.rings[0].start()
            if self.diagonal:
                send(self.ref.at[q], self.rings[1].k, dp)
                send(self.ref.at[q], self.rings[1].k + 1, dm)
            self.to_twin(zl, y)

        def other_half(self):
            wait_recv(self.ref.at[col_of(1 - zl, y, core)], self.k)
            if not self.diagonal:
                self.rings[1].start()
            self.to_twin(1 - zl, y)

        def from_minus(self, e):
            self.rings[e].from_minus()
            self.to_twin((zl, 1 - zl)[e], y - 1)

        def from_plus(self, e):
            self.rings[e].from_plus()
            self.to_twin((zl, 1 - zl)[e], y + 1)

        def finish(self, e):
            self.rings[e].finish()
            self.to_twin((zl, 1 - zl)[e], y + 2)

        def finish_twin(self):
            for n, (ll, at) in enumerate(self.passed):
                wait_recv(self.ref.at[col_of(ll, at, 1 - core)], self.k + 9 + n)

        def drain(self):
            wait_send(self.ref.at[q], self.k)
            for ring in self.rings:
                ring.drain()
            for n, (ll, at) in enumerate(self.passed):
                wait_send(self.ref.at[col_of(ll, at, core)], self.k + 9 + n)

    class Rows:
        def __init__(self, block, half, k):
            self.zring = Ring(
                lambda zz: block(zz, x), lambda zz, h: half(zz, x, h), z, zp, zm, k
            )

            def slot(zz):
                return lambda xx: block(zz, xx)

            def part(zz):
                return lambda xx, h: half(zz, xx, h)

            self.order = [z, lax.rem(z + 3, 4), lax.rem(z + 1, 4), lax.rem(z + 2, 4)]
            self.xrings = [
                Ring(slot(zz), part(zz), x, xp, xm, k + 4 + 4 * e)
                for e, zz in enumerate(self.order)
            ]

        def start(self):
            self.zring.start()
            self.xrings[0].start()

        def z_neighbours(self):
            self.zring.from_minus()
            self.xrings[1].start()
            self.zring.from_plus()
            self.xrings[2].start()

        def z_far(self):
            self.zring.finish()
            self.xrings[3].start()

        def x_neighbours(self, e):
            self.xrings[e].from_minus()
            self.xrings[e].from_plus()

        def x_far(self, e):
            self.xrings[e].finish()

        def drain(self):
            self.zring.drain()
            for ring in self.xrings:
                ring.drain()

    def right_rows(zz, xx, h, count):
        return pl.ds(pl.multiple_of((xx * 4 + zz) * 32 + 16 * h, 16), count)

    right_rows_gather = Rows(
        lambda zz, xx: right_all.at[right_rows(zz, xx, 0, 32)],
        lambda zz, xx, h: right_all.at[right_rows(zz, xx, h, 16)],
        RIGHT_GATHER,
    )
    left_columns = Columns(left_all, 2, LEFT_GATHER, True)

    def zero_chunk(t, carry):
        bd[pl.ds(pl.multiple_of(t * 128, 128), 128), :] = jnp.zeros((128, 512), BF16)
        part[pl.ds(pl.multiple_of(t * 144, 144), 144), :] = jnp.zeros((144, 128), F32)
        return carry

    lax.fori_loop(0, 32, zero_chunk, 0)
    loads["oproj"].wait()

    def fill_chunk(t, carry):
        block = oproj_ref[pl.ds(pl.multiple_of(t * 32, 32), 32), :]
        for u in range(4):
            bd[pl.ds(pl.multiple_of(t * 128 + 32 * u, 32), 32), 128 * u : 128 * u + 128] = block
        return carry

    lax.fori_loop(0, 32, fill_chunk, 0)
    loads["rmask"].wait()
    mask_k = jnp.zeros((24, 128), F32)
    sub = lax.broadcasted_iota(I32, (24, 128), 0)
    for k in range(24):
        mask_k = jnp.where(sub == k, rmask_ref[q * 24 + k].astype(F32), mask_k)
    for i in range(24):
        pmask[24 * i : 24 * i + 24, :] = mask_k * rmask_ref[r * 24 + i].astype(F32)
    for name in ("pair", "tproj", "tgate", "tout", "tin", "trans"):
        loads[name].wait()

    pl.semaphore_wait(barrier, 18 - 2 * same.astype(I32))

    def scatter(t, carry):
        is_self = same & (t == z)
        p = t * 4 + x

        @pl.when(jnp.logical_not(is_self))
        def _():
            remote(
                left_send.at[t], left_all.at[p, z], LEFT_SCATTER + t, LEFT_SCATTER + z, (q, p)
            ).start()

        @pl.when(is_self)
        def _():
            left_all[p, z] = left_send[t]

        return carry

    lax.fori_loop(0, 4, scatter, 0)
    right_rows_gather.start()

    def scatter_arrived(t, carry):
        @pl.when(jnp.logical_not(same & (t == z)))
        def _():
            piece = left_all.at[q, t]
            remote(piece, piece, LEFT_SCATTER + t, LEFT_SCATTER + t, twin).wait_recv()

        return carry

    lax.fori_loop(0, 4, scatter_arrived, 0)
    left_columns.start()
    right_rows_gather.z_neighbours()
    right_rows_gather.x_neighbours(0)
    left_columns.other_half()
    for e in range(2):
        left_columns.from_minus(e)
        left_columns.from_plus(e)
    right_rows_gather.z_far()
    right_rows_gather.x_neighbours(1)
    right_rows_gather.x_neighbours(2)
    left_columns.finish(0)
    left_columns.finish(1)
    right_rows_gather.x_neighbours(3)
    left_columns.finish_twin()

    for g in range(6):
        for m in range(4):
            left_t[128 * g : 128 * g + 128, 128 * m : 128 * m + 128] = (
                left_all[4 * (g // 2) + m, :, g % 2].reshape(128, 128).T
            )
    for e in range(4):
        right_rows_gather.x_far(e)

    counts = sum(
        dot(
            left_all[12 + m, :, 0].reshape(128, 128).T,
            right_all[128 * m : 128 * m + 128, 768:896],
        )
        for m in range(4)
    )
    counts = jnp.maximum(counts[:24], 1.0)
    for g in range(3):
        outer = dot(left_t[...], right_all[:, 256 * g : 256 * g + 256])
        for u in range(2):
            for c in range(32):
                lhs2[32 * (2 * g + u) : 32 * (2 * g + u) + 24, 128 * c : 128 * c + 128] = outer[
                    24 * c : 24 * c + 24, 128 * u : 128 * u + 128
                ].astype(BF16)
    for n in range(2):
        proj = dot(lhs2[...], bd[:, 256 * n : 256 * n + 256])
        for g in range(6):
            for u in range(2):
                j = 4 * g + 2 * n + u
                ptile[24 * j : 24 * j + 24, :] = (
                    proj[32 * g : 32 * g + 24, 128 * u : 128 * u + 128] / counts[:, j : j + 1]
                )
    for i in range(0, 24, 2):
        rows = slice(24 * i, 24 * i + 48)
        tiles = [ptile[pl.ds(i + v, 24, stride=24), :] for v in range(2)]
        rounded = (pair_ref[rows, :].astype(F32) + jnp.concatenate(tiles, axis=0)).astype(BF16)
        rounded = rounded.astype(F32)
        first[rows, :] = rounded
        normed[rows, :] = norm(rounded).astype(BF16)

    for t in range(3):
        rows = slice(192 * t, 192 * t + 192)
        p = dot(normed[rows, :], tproj_ref[...])
        m = pmask[rows, :]
        tri_left[q, rows, :] = (jax.nn.sigmoid(p[:, :128]) * p[:, 128:256] * m).astype(BF16)
        tri_send[rows, :] = (jax.nn.sigmoid(p[:, 256:384]) * p[:, 384:] * m).astype(BF16)

    tri_columns = Columns(tri_left, 288, TRI_LEFT, False)

    def chunk(n):
        return Rows(
            lambda zz, xx: tri_right.at[xx, zz, pl.ds(2 * n, 2)],
            lambda zz, xx, h: tri_right.at[xx, zz, pl.ds(2 * n + h, 1)],
            TRI_RIGHT + 20 * n,
        )

    rows0, rows1 = chunk(0), chunk(1)
    holder, place = lax.rem(q, 4), q // 4

    def tri_scatter(t, carry):
        is_self = same & (t == z)
        piece = pl.ds(pl.multiple_of(t * 144, 144), 144)

        @pl.when(jnp.logical_not(is_self))
        def _():
            remote(
                tri_send.at[piece], tri_right.at[holder, t, place], TRI_SCATTER + t,
                TRI_SCATTER + place, (t * 4 + holder, r),
            ).start()

        @pl.when(is_self)
        def _():
            tri_right[holder, t, place] = tri_send[piece, :]

        return carry

    lax.fori_loop(0, 4, tri_scatter, 0)
    tri_columns.start()

    def tri_arrived(t, carry):
        @pl.when(jnp.logical_not(same & (t == place)))
        def _():
            piece = tri_right.at[x, z, t]
            remote(piece, piece, TRI_SCATTER + t, TRI_SCATTER + t, twin).wait_recv()

        return carry

    lax.fori_loop(0, 4, tri_arrived, 0)
    rows0.start()
    rows1.start()
    tri_columns.other_half()

    gate[...] = jax.nn.sigmoid(dot(normed[...], tgate_ref[...]))

    def widen_left(xx):
        def widen(t, carry):
            b, rows = t // 4, pl.ds(pl.multiple_of(lax.rem(t, 4) * 144, 144), 144)
            lf[xx, b, rows, :] = tri_left[b * 4 + xx, rows, :].astype(F32)
            return carry

        lax.fori_loop(0, 16, widen, 0)

    def accumulate(xx, zz):
        def widen(t, carry):
            rf[t] = tri_right[xx, zz, t].astype(F32)
            return carry

        lax.fori_loop(0, 4, widen, 0)

        def block(t, carry):
            def at(u, v):
                return pl.ds(pl.multiple_of(((t * 4 + u) * 24 + zz * 6 + v) * 8, 8), 8)

            acc = [[part[at(u, v), :] for v in range(6)] for u in range(4)]
            for b in range(4):
                for k in range(3):
                    left = [
                        lf[xx, b, pl.ds(pl.multiple_of((t * 4 + u) * 24 + 8 * k, 8), 8), :]
                        for u in range(4)
                    ]
                    right = [rf[b, 24 * v + 8 * k : 24 * v + 8 * k + 8, :] for v in range(6)]
                    for u in range(4):
                        for v in range(6):
                            acc[u][v] = acc[u][v] + left[u] * right[v]
            for u in range(4):
                for v in range(6):
                    part[at(u, v), :] = acc[u][v]
            return carry

        lax.fori_loop(0, 6, block, 0)

    def xat(d):
        return lax.rem(x + d + 4, 4)

    tri_columns.from_minus(0)
    tri_columns.from_plus(0)
    rows0.z_neighbours()
    rows0.x_neighbours(0)
    rows1.z_neighbours()
    rows1.x_neighbours(0)
    tri_columns.from_minus(1)
    tri_columns.from_plus(1)
    rows0.z_far()
    tri_columns.finish(0)
    rows0.x_neighbours(1)
    rows0.x_neighbours(2)
    rows1.z_far()
    tri_columns.finish(1)
    rows1.x_neighbours(1)
    tri_columns.finish_twin()
    order = rows0.order
    widen_left(x)
    accumulate(x, order[0])
    rows1.x_neighbours(2)
    rows0.x_neighbours(3)
    accumulate(x, order[1])
    accumulate(x, order[2])
    rows1.x_neighbours(3)
    accumulate(x, order[3])
    for d in (-1, 1):
        widen_left(xat(d))
    for e in range(4):
        for d in (-1, 1):
            accumulate(xat(d), order[e])
    widen_left(xat(2))
    for e in range(4):
        rows0.x_far(e)
        rows1.x_far(e)
        accumulate(xat(2), order[e])

    for t in range(2):
        rows = slice(288 * t, 288 * t + 288)
        summed = part[pl.ds(2304 * t, 288, stride=8), :]
        for k in range(1, 8):
            summed = summed + part[pl.ds(2304 * t + k, 288, stride=8), :]
        normed_sum = norm(summed).astype(BF16)
        second = (first[rows, :] + gate[rows, :] * dot(normed_sum, tout_ref[...])).astype(BF16)
        second = second.astype(F32)
        hidden = jnp.maximum(dot(norm(second).astype(BF16), tin_ref[...]), 0.0).astype(BF16)
        out_ref[rows, :] = (second + dot(hidden, trans_ref[...])).astype(BF16)

    def scatter_left(t, carry):
        @pl.when(jnp.logical_not(same & (t == z)))
        def _():
            remote(
                left_send.at[t], left_send.at[t], LEFT_SCATTER + t, LEFT_SCATTER + t, twin
            ).wait_send()

        return carry

    lax.fori_loop(0, 4, scatter_left, 0)

    def tri_left_here(t, carry):
        @pl.when(jnp.logical_not(same & (t == z)))
        def _():
            piece = tri_send.at[pl.ds(pl.multiple_of(t * 144, 144), 144)]
            remote(piece, piece, TRI_SCATTER + t, TRI_SCATTER + t, twin).wait_send()

        return carry

    lax.fori_loop(0, 4, tri_left_here, 0)
    left_columns.drain()
    right_rows_gather.drain()
    tri_columns.drain()
    rows0.drain()
    rows1.drain()


def shards(alignment, alignment_mask, residue_mask, pair_features, *weights):
    vmem = pl.BlockSpec(memory_space=pltpu.VMEM)
    hbm = pl.BlockSpec(memory_space=pltpu.HBM)
    out = pl.pallas_call(
        kernel,
        out_shape=jax.ShapeDtypeStruct((576, 128), BF16),
        in_specs=[hbm] * 12,
        out_specs=vmem,
        scratch_shapes=[
            pltpu.VMEM((768, 256), BF16),
            pltpu.VMEM((24, 32), I32),
            pltpu.SMEM((384,), I32),
            pltpu.VMEM((576, 128), BF16),
            pltpu.VMEM((32, 256), BF16),
            pltpu.VMEM((32, 256), BF16),
            pltpu.VMEM((1024, 128), BF16),
            pltpu.VMEM((128, 512), BF16),
            pltpu.VMEM((128, 128), BF16),
            pltpu.VMEM((128, 128), BF16),
            pltpu.VMEM((128, 512), BF16),
            pltpu.VMEM((512, 128), BF16),
            pltpu.VMEM((2, 768, 128), F32),
            pltpu.VMEM((1024, 256), BF16),
            pltpu.VMEM((768, 768), BF16),
            pltpu.VMEM((4096, 512), BF16),
            pltpu.VMEM((32, 768), BF16),
            pltpu.VMEM((4, 2, 32, 128), BF16),
            pltpu.VMEM((16, 4, 2, 32, 128), BF16),
            pltpu.VMEM((512, 896), BF16),
            pltpu.VMEM((768, 512), BF16),
            pltpu.VMEM((192, 4096), BF16),
            pltpu.VMEM((576, 128), F32),
            pltpu.VMEM((576, 128), F32),
            pltpu.VMEM((576, 128), BF16),
            pltpu.VMEM((576, 128), F32),
            pltpu.VMEM((576, 128), F32),
            pltpu.VMEM((16, 576, 128), BF16),
            pltpu.VMEM((576, 128), BF16),
            pltpu.VMEM((4, 4, 4, 144, 128), BF16),
            pltpu.VMEM((4, 4, 576, 128), F32),
            pltpu.VMEM((4, 144, 128), F32),
            pltpu.VMEM((4608, 128), F32),
            pltpu.SemaphoreType.DMA((TRANSFERS,)),
            pltpu.SemaphoreType.DMA((TRANSFERS,)),
            pltpu.SemaphoreType.DMA((12,)),
        ],
        compiler_params=pltpu.CompilerParams(
            collective_id=0, has_side_effects=True, vmem_limit_bytes=60 * 1024 * 1024
        ),
        cost_estimate=pl.CostEstimate(
            flops=1_500_000_000, bytes_accessed=2_000_000, transcendentals=400_000
        ),
    )(
        alignment.reshape(768, 256), alignment_mask.T, residue_mask, pair_features.reshape(576, 128),
        weights[0].T, weights[1].T, *weights[2:],
    )
    return out.reshape(24, 24, 128)


def solution(mesh):
    placed = (P("row", "col", None), P("row", "col"), P(), P("row", "col", None)) + (P(),) * 8
    return jax.shard_map(
        shards, mesh=mesh, in_specs=placed, out_specs=P("row", "col", None), check_vma=False
    )
```

```python
import jax
import jax.numpy as jnp
from jax import lax
from jax.experimental import pallas as pl
from jax.experimental.pallas import tpu as pltpu
from jax.sharding import PartitionSpec as P

EPSILON = 1e-05
MESH = pl.DeviceIdType.MESH
F32 = jnp.float32
BF16 = jnp.bfloat16
I32 = jnp.int32

LEFT_SCATTER = 0
LEFT_GATHER = 4
RIGHT_GATHER = 21
TRI_SCATTER = 41
TRI_LEFT = 45
TRI_RIGHT = 62
TRANSFERS = 102


def norm(v):
    mean = jnp.mean(v, axis=-1, keepdims=True)
    centered = v - mean
    variance = jnp.mean(centered * centered, axis=-1, keepdims=True)
    return centered * lax.rsqrt(variance + EPSILON)


def dot(a, b):
    return jnp.dot(a, b, preferred_element_type=F32)


def kernel(
    align_hbm, amask_hbm, rmask_hbm, pair_hbm, wl_hbm, wr_hbm, oproj_hbm, tproj_hbm, tgate_hbm,
    tout_hbm, tin_hbm, trans_hbm, out_ref,
    align_ref, amask_ref, rmask_ref, pair_ref, wl_ref, wr_ref, oproj_ref, tproj_ref, tgate_ref,
    tout_ref, tin_ref, trans_ref,
    xs, wbd, perm, bd, lnat, left_send, left_all, right_all, left_t, lhs2, ptile, first, normed,
    pmask, gate, tri_left, tri_send, tri_right, lf, rf, part, ss, rs, ls,
):
    loads = {
        name: pltpu.make_async_copy(src, dst, ls.at[n])
        for n, (name, src, dst) in enumerate(
            (
                ("align", align_hbm, align_ref),
                ("wl", wl_hbm, wl_ref),
                ("wr", wr_hbm, wr_ref),
                ("amask", amask_hbm, amask_ref),
                ("oproj", oproj_hbm, oproj_ref),
                ("rmask", rmask_hbm, rmask_ref),
                ("pair", pair_hbm, pair_ref),
                ("tproj", tproj_hbm, tproj_ref),
                ("tgate", tgate_hbm, tgate_ref),
                ("tout", tout_hbm, tout_ref),
                ("tin", tin_hbm, tin_ref),
                ("trans", trans_hbm, trans_ref),
            )
        )
    }
    r, q = lax.axis_index("row"), lax.axis_index("col")
    z, x = r // 4, lax.rem(r, 4)
    zl, y, core = q // 8, lax.rem(q // 2, 4), lax.rem(q, 2)
    same = r == q

    def row_of(zz, xx):
        return lax.rem(zz + 4, 4) * 4 + lax.rem(xx + 4, 4)

    def col_of(ll, yy, cc):
        return (ll * 4 + lax.rem(yy + 4, 4)) * 2 + cc

    zp, zm = (row_of(z + 1, x), q), (row_of(z - 1, x), q)
    xp, xm = (row_of(z, x + 1), q), (row_of(z, x - 1), q)
    yp, ym = (r, col_of(zl, y + 1, core)), (r, col_of(zl, y - 1, core))
    zlo = (r, col_of(1 - zl, y, core))
    twin = (r, col_of(zl, y, 1 - core))
    dp, dm = (r, col_of(1 - zl, y + 1, core)), (r, col_of(1 - zl, y - 1, core))

    barrier = pltpu.get_barrier_semaphore()
    def greet(t, carry):
        @pl.when(jnp.logical_not(same & (t == z)))
        def _():
            pl.semaphore_signal(
                barrier, inc=1, device_id=(t * 4 + lax.rem(q, 4), r), device_id_type=MESH
            )

        return carry

    for t in range(4):
        greet(t, 0)

    def greet_tri(t, carry):
        @pl.when(jnp.logical_not(same & (t * 4 + x == q)))
        def _():
            pl.semaphore_signal(barrier, inc=1, device_id=(q, t * 4 + x), device_id_type=MESH)

        return carry

    for t in range(4):
        greet_tri(t, 0)
    for device in (zp, zm, xp, xm, yp, ym, zlo, twin, dp, dm):
        pl.semaphore_signal(barrier, inc=1, device_id=device, device_id_type=MESH)

    for load in loads.values():
        load.start()

    loads["align"].wait()

    def norm_chunk(t, carry):
        rows = pl.ds(pl.multiple_of(t * 96, 96), 96)
        v = norm(align_ref[rows, :].astype(F32))
        xs[0, rows, :] = v[:, :128]
        xs[1, rows, :] = v[:, 128:]
        return carry

    lax.fori_loop(0, 8, norm_chunk, 0)

    lane = lax.broadcasted_iota(I32, (256, 128), 1)
    spread = (
        lax.rem(lax.broadcasted_iota(I32, (32, 128), 1), 32)
        == lax.broadcasted_iota(I32, (32, 128), 0)
    ).astype(F32).astype(BF16)
    loads["wl"].wait()
    loads["wr"].wait()
    for side, w_ref in enumerate((wl_ref, wr_ref)):
        w = dot(w_ref[...].astype(F32).T.astype(BF16), spread)
        for u in range(4):
            own = (lane >= 32 * u) & (lane < 32 * u + 32)
            wbd[256 * u : 256 * u + 256, 128 * side : 128 * side + 128] = jnp.where(
                own, w, 0.0
            ).astype(BF16)

    lam = lax.broadcasted_iota(I32, (1, 768), 1)
    by24 = (lam * 2731) // 65536
    target = (lam - by24 * 24) * 32 + by24

    def perm_chunk(t, carry):
        start = pl.multiple_of(t * 64, 64)
        rows = lax.broadcasted_iota(I32, (64, 768), 0) + start
        perm[pl.ds(start, 64), :] = (rows == target).astype(F32).astype(BF16)
        return carry

    lax.fori_loop(0, 12, perm_chunk, 0)

    loads["amask"].wait()
    amask = amask_ref[...].astype(F32).T.astype(BF16)
    row24 = lax.broadcasted_iota(I32, (24, 768), 0) * 32
    lane24 = lax.broadcasted_iota(I32, (24, 768), 1)
    expand = ((lane24 >= row24) & (lane24 < row24 + 32)).astype(F32).astype(BF16)
    mask_wide = dot(amask, expand)
    mask_lanes = dot(
        amask,
        (
            lax.broadcasted_iota(I32, (24, 128), 0) == lax.broadcasted_iota(I32, (24, 128), 1)
        ).astype(F32).astype(BF16),
    ).astype(BF16)
    own_rows = pl.ds(pl.multiple_of((x * 4 + z) * 32, 32), 32)
    for g in range(6):
        four = jnp.concatenate(
            [
                xs[half, pl.ds(4 * g + u, 32, stride=24), :].astype(BF16)
                for u in range(4)
                for half in range(2)
            ],
            axis=1,
        )
        both = dot(four, wbd[...])
        m = mask_wide[:, 128 * g : 128 * g + 128]
        lnat[:, 128 * g : 128 * g + 128] = (both[:, :128] * m).astype(BF16)
        right = (both[:, 128:] * m).astype(BF16)
        right_all[own_rows, 128 * g : 128 * g + 128] = right
    left = dot(lnat[...], perm[...]).astype(BF16)
    right_all[own_rows, 768:896] = mask_lanes
    for g in range(6):
        left_send[g // 2, g % 2] = left[:, 128 * g : 128 * g + 128]
    left_send[3, 0] = mask_lanes
    left_send[3, 1] = jnp.zeros((32, 128), BF16)

    def remote(src, dst, send, recv, device):
        return pltpu.make_async_remote_copy(
            src_ref=src, dst_ref=dst, send_sem=ss.at[send], recv_sem=rs.at[recv],
            device_id=device, device_id_type=MESH,
        )

    def send(ref, k, device):
        remote(ref, ref, k, k, device).start()

    def wait_recv(ref, k):
        remote(ref, ref, k, k, twin).wait_recv()

    def wait_send(ref, k):
        remote(ref, ref, k, k, twin).wait_send()

    class Ring:
        def __init__(self, slot, half, at, plus, minus, k):
            self.slot, self.half, self.at = slot, half, at
            self.plus, self.minus, self.k = plus, minus, k

        def pos(self, d):
            return lax.rem(self.at + d + 4, 4)

        def start(self):
            send(self.slot(self.at), self.k, self.plus)
            send(self.slot(self.at), self.k + 1, self.minus)

        def from_minus(self):
            wait_recv(self.slot(self.pos(-1)), self.k)
            send(self.half(self.pos(-1), 0), self.k + 2, self.plus)

        def from_plus(self):
            wait_recv(self.slot(self.pos(1)), self.k + 1)
            send(self.half(self.pos(1), 1), self.k + 3, self.minus)

        def finish(self):
            wait_recv(self.half(self.pos(2), 0), self.k + 2)
            wait_recv(self.half(self.pos(2), 1), self.k + 3)

        def drain(self):
            wait_send(self.slot(self.at), self.k)
            wait_send(self.slot(self.at), self.k + 1)
            wait_send(self.half(self.pos(-1), 0), self.k + 2)
            wait_send(self.half(self.pos(1), 1), self.k + 3)

    class Columns:
        def __init__(self, ref, half_rows, k, diagonal):
            self.ref, self.k, self.diagonal = ref, k, diagonal

            def slot(ll):
                return lambda yy: ref.at[col_of(ll, yy, core)]

            def half(ll):
                return lambda yy, h: ref.at[
                    col_of(ll, yy, core), pl.ds(h * half_rows, half_rows)
                ]

            self.rings = [
                Ring(slot(ll), half(ll), y, yp, ym, k + 1 + 4 * e)
                for e, ll in enumerate((zl, 1 - zl))
            ]
            self.passed = []

        def to_twin(self, ll, yy):
            n = len(self.passed)
            at = lax.rem(yy + 4, 4)
            self.passed.append((ll, at))
            send(self.ref.at[col_of(ll, at, core)], self.k + 9 + n, twin)

        def start(self):
            send(self.ref.at[q], self.k, zlo)
            self.rings[0].start()
            if self.diagonal:
                send(self.ref.at[q], self.rings[1].k, dp)
                send(self.ref.at[q], self.rings[1].k + 1, dm)
            self.to_twin(zl, y)

        def other_half(self):
            wait_recv(self.ref.at[col_of(1 - zl, y, core)], self.k)
            if not self.diagonal:
                self.rings[1].start()
            self.to_twin(1 - zl, y)

        def from_minus(self, e):
            self.rings[e].from_minus()
            self.to_twin((zl, 1 - zl)[e], y - 1)

        def from_plus(self, e):
            self.rings[e].from_plus()
            self.to_twin((zl, 1 - zl)[e], y + 1)

        def finish(self, e):
            self.rings[e].finish()
            self.to_twin((zl, 1 - zl)[e], y + 2)

        def finish_twin(self):
            for n, (ll, at) in enumerate(self.passed):
                wait_recv(self.ref.at[col_of(ll, at, 1 - core)], self.k + 9 + n)

        def drain(self):
            wait_send(self.ref.at[q], self.k)
            for ring in self.rings:
                ring.drain()
            for n, (ll, at) in enumerate(self.passed):
                wait_send(self.ref.at[col_of(ll, at, core)], self.k + 9 + n)

    class Rows:
        def __init__(self, block, half, k):
            self.zring = Ring(
                lambda zz: block(zz, x), lambda zz, h: half(zz, x, h), z, zp, zm, k
            )

            def slot(zz):
                return lambda xx: block(zz, xx)

            def part(zz):
                return lambda xx, h: half(zz, xx, h)

            self.order = [z, lax.rem(z + 3, 4), lax.rem(z + 1, 4), lax.rem(z + 2, 4)]
            self.xrings = [
                Ring(slot(zz), part(zz), x, xp, xm, k + 4 + 4 * e)
                for e, zz in enumerate(self.order)
            ]

        def start(self):
            self.zring.start()
            self.xrings[0].start()

        def z_neighbours(self):
            self.zring.from_minus()
            self.xrings[1].start()
            self.zring.from_plus()
            self.xrings[2].start()

        def z_far(self):
            self.zring.finish()
            self.xrings[3].start()

        def x_neighbours(self, e):
            self.xrings[e].from_minus()
            self.xrings[e].from_plus()

        def x_far(self, e):
            self.xrings[e].finish()

        def drain(self):
            self.zring.drain()
            for ring in self.xrings:
                ring.drain()

    def right_rows(zz, xx, h, count):
        return pl.ds(pl.multiple_of((xx * 4 + zz) * 32 + 16 * h, 16), count)

    right_rows_gather = Rows(
        lambda zz, xx: right_all.at[right_rows(zz, xx, 0, 32)],
        lambda zz, xx, h: right_all.at[right_rows(zz, xx, h, 16)],
        RIGHT_GATHER,
    )
    left_columns = Columns(left_all, 2, LEFT_GATHER, True)

    def zero_chunk(t, carry):
        bd[pl.ds(pl.multiple_of(t * 128, 128), 128), :] = jnp.zeros((128, 512), BF16)
        part[pl.ds(pl.multiple_of(t * 144, 144), 144), :] = jnp.zeros((144, 128), F32)
        return carry

    lax.fori_loop(0, 32, zero_chunk, 0)
    loads["oproj"].wait()

    def fill_chunk(t, carry):
        block = oproj_ref[pl.ds(pl.multiple_of(t * 32, 32), 32), :]
        for u in range(4):
            bd[pl.ds(pl.multiple_of(t * 128 + 32 * u, 32), 32), 128 * u : 128 * u + 128] = block
        return carry

    lax.fori_loop(0, 32, fill_chunk, 0)
    loads["rmask"].wait()
    mask_k = jnp.zeros((24, 128), F32)
    sub = lax.broadcasted_iota(I32, (24, 128), 0)
    for k in range(24):
        mask_k = jnp.where(sub == k, rmask_ref[q * 24 + k].astype(F32), mask_k)
    for i in range(24):
        pmask[24 * i : 24 * i + 24, :] = mask_k * rmask_ref[r * 24 + i].astype(F32)
    for name in ("pair", "tproj", "tgate", "tout", "tin", "trans"):
        loads[name].wait()

    pl.semaphore_wait(barrier, 18 - 2 * same.astype(I32))

    def scatter(t, carry):
        is_self = same & (t == z)
        p = t * 4 + x

        @pl.when(jnp.logical_not(is_self))
        def _():
            remote(
                left_send.at[t], left_all.at[p, z], LEFT_SCATTER + t, LEFT_SCATTER + z, (q, p)
            ).start()

        @pl.when(is_self)
        def _():
            left_all[p, z] = left_send[t]

        return carry

    lax.fori_loop(0, 4, scatter, 0)
    right_rows_gather.start()

    def scatter_arrived(t, carry):
        @pl.when(jnp.logical_not(same & (t == z)))
        def _():
            piece = left_all.at[q, t]
            remote(piece, piece, LEFT_SCATTER + t, LEFT_SCATTER + t, twin).wait_recv()

        return carry

    lax.fori_loop(0, 4, scatter_arrived, 0)
    left_columns.start()
    right_rows_gather.z_neighbours()
    left_columns.other_half()
    left_columns.from_minus(0)
    left_columns.from_plus(0)
    right_rows_gather.x_neighbours(0)
    right_rows_gather.z_far()
    left_columns.from_minus(1)
    left_columns.from_plus(1)
    right_rows_gather.x_neighbours(1)
    right_rows_gather.x_neighbours(2)
    left_columns.finish(0)
    right_rows_gather.x_neighbours(3)
    left_columns.finish(1)
    left_columns.finish_twin()

    for g in range(6):
        for m in range(4):
            left_t[128 * g : 128 * g + 128, 128 * m : 128 * m + 128] = (
                left_all[4 * (g // 2) + m, :, g % 2].reshape(128, 128).T
            )
    for e in range(4):
        right_rows_gather.x_far(e)

    counts = sum(
        dot(
            left_all[12 + m, :, 0].reshape(128, 128).T,
            right_all[128 * m : 128 * m + 128, 768:896],
        )
        for m in range(4)
    )
    counts = jnp.maximum(counts[:24], 1.0)
    for g in range(3):
        outer = dot(left_t[...], right_all[:, 256 * g : 256 * g + 256])
        for u in range(2):
            for c in range(32):
                lhs2[32 * (2 * g + u) : 32 * (2 * g + u) + 24, 128 * c : 128 * c + 128] = outer[
                    24 * c : 24 * c + 24, 128 * u : 128 * u + 128
                ].astype(BF16)
    for n in range(2):
        proj = dot(lhs2[...], bd[:, 256 * n : 256 * n + 256])
        for g in range(6):
            for u in range(2):
                j = 4 * g + 2 * n + u
                ptile[24 * j : 24 * j + 24, :] = (
                    proj[32 * g : 32 * g + 24, 128 * u : 128 * u + 128] / counts[:, j : j + 1]
                )
    for i in range(0, 24, 2):
        rows = slice(24 * i, 24 * i + 48)
        tiles = [ptile[pl.ds(i + v, 24, stride=24), :] for v in range(2)]
        rounded = (pair_ref[rows, :].astype(F32) + jnp.concatenate(tiles, axis=0)).astype(BF16)
        rounded = rounded.astype(F32)
        first[rows, :] = rounded
        normed[rows, :] = norm(rounded).astype(BF16)

    for t in range(3):
        rows = slice(192 * t, 192 * t + 192)
        p = dot(normed[rows, :], tproj_ref[:, 256:])
        tri_send[rows, :] = (jax.nn.sigmoid(p[:, :128]) * p[:, 128:] * pmask[rows, :]).astype(BF16)

    tri_columns = Columns(tri_left, 288, TRI_LEFT, False)

    def chunk(n):
        return Rows(
            lambda zz, xx: tri_right.at[xx, zz, pl.ds(2 * n, 2)],
            lambda zz, xx, h: tri_right.at[xx, zz, pl.ds(2 * n + h, 1)],
            TRI_RIGHT + 20 * n,
        )

    rows0, rows1 = chunk(0), chunk(1)
    holder, place = lax.rem(q, 4), q // 4

    def tri_scatter(t, carry):
        is_self = same & (t == z)
        piece = pl.ds(pl.multiple_of(t * 144, 144), 144)

        @pl.when(jnp.logical_not(is_self))
        def _():
            remote(
                tri_send.at[piece], tri_right.at[holder, t, place], TRI_SCATTER + t,
                TRI_SCATTER + place, (t * 4 + holder, r),
            ).start()

        @pl.when(is_self)
        def _():
            tri_right[holder, t, place] = tri_send[piece, :]

        return carry

    lax.fori_loop(0, 4, tri_scatter, 0)
    for t in range(3):
        rows = slice(192 * t, 192 * t + 192)
        p = dot(normed[rows, :], tproj_ref[:, :256])
        tri_left[q, rows, :] = (
            jax.nn.sigmoid(p[:, :128]) * p[:, 128:] * pmask[rows, :]
        ).astype(BF16)
    tri_columns.start()

    def tri_arrived(t, carry):
        @pl.when(jnp.logical_not(same & (t == place)))
        def _():
            piece = tri_right.at[x, z, t]
            remote(piece, piece, TRI_SCATTER + t, TRI_SCATTER + t, twin).wait_recv()

        return carry

    lax.fori_loop(0, 4, tri_arrived, 0)
    rows0.start()
    rows1.start()
    tri_columns.other_half()

    gate[...] = jax.nn.sigmoid(dot(normed[...], tgate_ref[...]))

    def widen_left(xx):
        def widen(t, carry):
            b, rows = t // 4, pl.ds(pl.multiple_of(lax.rem(t, 4) * 144, 144), 144)
            lf[xx, b, rows, :] = tri_left[b * 4 + xx, rows, :].astype(F32)
            return carry

        lax.fori_loop(0, 16, widen, 0)

    def accumulate(xx, zz):
        def widen(t, carry):
            rf[t] = tri_right[xx, zz, t].astype(F32)
            return carry

        lax.fori_loop(0, 4, widen, 0)

        def block(t, carry):
            def at(u, v):
                return pl.ds(pl.multiple_of(((t * 4 + u) * 24 + zz * 6 + v) * 8, 8), 8)

            acc = [[part[at(u, v), :] for v in range(6)] for u in range(4)]
            for b in range(4):
                for k in range(3):
                    left = [
                        lf[xx, b, pl.ds(pl.multiple_of((t * 4 + u) * 24 + 8 * k, 8), 8), :]
                        for u in range(4)
                    ]
                    right = [rf[b, 24 * v + 8 * k : 24 * v + 8 * k + 8, :] for v in range(6)]
                    for u in range(4):
                        for v in range(6):
                            acc[u][v] = acc[u][v] + left[u] * right[v]
            for u in range(4):
                for v in range(6):
                    part[at(u, v), :] = acc[u][v]
            return carry

        lax.fori_loop(0, 6, block, 0)

    def xat(d):
        return lax.rem(x + d + 4, 4)

    tri_columns.from_minus(0)
    tri_columns.from_plus(0)
    rows0.z_neighbours()
    rows0.x_neighbours(0)
    tri_columns.from_minus(1)
    tri_columns.from_plus(1)
    rows1.z_neighbours()
    rows1.x_neighbours(0)
    tri_columns.finish(0)
    rows0.z_far()
    tri_columns.finish(1)
    rows0.x_neighbours(1)
    rows0.x_neighbours(2)
    tri_columns.finish_twin()
    order = rows0.order
    widen_left(x)
    accumulate(x, order[0])
    rows1.z_far()
    rows1.x_neighbours(1)
    accumulate(x, order[1])
    rows1.x_neighbours(2)
    accumulate(x, order[2])
    accumulate(x, order[3])
    for d in (-1, 1):
        widen_left(xat(d))
    accumulate(xat(-1), order[0])
    rows0.x_neighbours(3)
    accumulate(xat(1), order[0])
    accumulate(xat(-1), order[1])
    rows1.x_neighbours(3)
    accumulate(xat(1), order[1])
    accumulate(xat(-1), order[2])
    accumulate(xat(1), order[2])
    widen_left(xat(2))
    for e in range(3):
        rows0.x_far(e)
        rows1.x_far(e)
        accumulate(xat(2), order[e])
    accumulate(xat(-1), order[3])
    accumulate(xat(1), order[3])
    rows0.x_far(3)
    rows1.x_far(3)
    accumulate(xat(2), order[3])

    for t in range(1):
        rows = slice(576 * t, 576 * t + 576)
        summed = part[pl.ds(2304 * t, 576, stride=8), :]
        for k in range(1, 8):
            summed = summed + part[pl.ds(2304 * t + k, 576, stride=8), :]
        normed_sum = norm(summed).astype(BF16)
        second = (first[rows, :] + gate[rows, :] * dot(normed_sum, tout_ref[...])).astype(BF16)
        second = second.astype(F32)
        hidden = jnp.maximum(dot(norm(second).astype(BF16), tin_ref[...]), 0.0).astype(BF16)
        out_ref[rows, :] = (second + dot(hidden, trans_ref[...])).astype(BF16)

    def scatter_left(t, carry):
        @pl.when(jnp.logical_not(same & (t == z)))
        def _():
            remote(
                left_send.at[t], left_send.at[t], LEFT_SCATTER + t, LEFT_SCATTER + t, twin
            ).wait_send()

        return carry

    lax.fori_loop(0, 4, scatter_left, 0)

    def tri_left_here(t, carry):
        @pl.when(jnp.logical_not(same & (t == z)))
        def _():
            piece = tri_send.at[pl.ds(pl.multiple_of(t * 144, 144), 144)]
            remote(piece, piece, TRI_SCATTER + t, TRI_SCATTER + t, twin).wait_send()

        return carry

    lax.fori_loop(0, 4, tri_left_here, 0)
    left_columns.drain()
    right_rows_gather.drain()
    tri_columns.drain()
    rows0.drain()
    rows1.drain()


def shards(alignment, alignment_mask, residue_mask, pair_features, *weights):
    vmem = pl.BlockSpec(memory_space=pltpu.VMEM)
    hbm = pl.BlockSpec(memory_space=pltpu.HBM)
    out = pl.pallas_call(
        kernel,
        out_shape=jax.ShapeDtypeStruct((576, 128), BF16),
        in_specs=[hbm] * 12,
        out_specs=vmem,
        scratch_shapes=[
            pltpu.VMEM((768, 256), BF16),
            pltpu.VMEM((24, 32), I32),
            pltpu.SMEM((384,), I32),
            pltpu.VMEM((576, 128), BF16),
            pltpu.VMEM((32, 256), BF16),
            pltpu.VMEM((32, 256), BF16),
            pltpu.VMEM((1024, 128), BF16),
            pltpu.VMEM((128, 512), BF16),
            pltpu.VMEM((128, 128), BF16),
            pltpu.VMEM((128, 128), BF16),
            pltpu.VMEM((128, 512), BF16),
            pltpu.VMEM((512, 128), BF16),
            pltpu.VMEM((2, 768, 128), F32),
            pltpu.VMEM((1024, 256), BF16),
            pltpu.VMEM((768, 768), BF16),
            pltpu.VMEM((4096, 512), BF16),
            pltpu.VMEM((32, 768), BF16),
            pltpu.VMEM((4, 2, 32, 128), BF16),
            pltpu.VMEM((16, 4, 2, 32, 128), BF16),
            pltpu.VMEM((512, 896), BF16),
            pltpu.VMEM((768, 512), BF16),
            pltpu.VMEM((192, 4096), BF16),
            pltpu.VMEM((576, 128), F32),
            pltpu.VMEM((576, 128), F32),
            pltpu.VMEM((576, 128), BF16),
            pltpu.VMEM((576, 128), F32),
            pltpu.VMEM((576, 128), F32),
            pltpu.VMEM((16, 576, 128), BF16),
            pltpu.VMEM((576, 128), BF16),
            pltpu.VMEM((4, 4, 4, 144, 128), BF16),
            pltpu.VMEM((4, 4, 576, 128), F32),
            pltpu.VMEM((4, 144, 128), F32),
            pltpu.VMEM((4608, 128), F32),
            pltpu.SemaphoreType.DMA((TRANSFERS,)),
            pltpu.SemaphoreType.DMA((TRANSFERS,)),
            pltpu.SemaphoreType.DMA((12,)),
        ],
        compiler_params=pltpu.CompilerParams(
            collective_id=0, has_side_effects=True, vmem_limit_bytes=60 * 1024 * 1024
        ),
        cost_estimate=pl.CostEstimate(
            flops=1_500_000_000, bytes_accessed=2_000_000, transcendentals=400_000
        ),
    )(
        alignment.reshape(768, 256), alignment_mask.T, residue_mask, pair_features.reshape(576, 128),
        weights[0].T, weights[1].T, *weights[2:],
    )
    return out.reshape(24, 24, 128)


def solution(mesh):
    placed = (P("row", "col", None), P("row", "col"), P(), P("row", "col", None)) + (P(),) * 8
    return jax.shard_map(
        shards, mesh=mesh, in_specs=placed, out_specs=P("row", "col", None), check_vma=False
    )
```

```python
import jax
import jax.numpy as jnp
from jax import lax
from jax.experimental import pallas as pl
from jax.experimental.pallas import tpu as pltpu
from jax.sharding import PartitionSpec as P

EPSILON = 1e-05
MESH = pl.DeviceIdType.MESH
F32 = jnp.float32
BF16 = jnp.bfloat16
I32 = jnp.int32

LEFT_SCATTER = 0
LEFT_GATHER = 4
RIGHT_GATHER = 21
TRI_SCATTER = 41
TRI_LEFT = 45
TRI_RIGHT = 62
TRANSFERS = 102


def norm(v):
    mean = jnp.mean(v, axis=-1, keepdims=True)
    centered = v - mean
    variance = jnp.mean(centered * centered, axis=-1, keepdims=True)
    return centered * lax.rsqrt(variance + EPSILON)


def dot(a, b):
    return jnp.dot(a, b, preferred_element_type=F32)


def kernel(
    align_hbm, amask_hbm, rmask_hbm, pair_hbm, wl_hbm, wr_hbm, oproj_hbm, tproj_hbm, tgate_hbm,
    tout_hbm, tin_hbm, trans_hbm, out_ref,
    align_ref, amask_ref, rmask_ref, pair_ref, wl_ref, wr_ref, oproj_ref, tproj_ref, tgate_ref,
    tout_ref, tin_ref, trans_ref,
    xs, wbd, perm, bd, lnat, left_send, left_all, right_all, left_t, lhs2, ptile, first, normed,
    pmask, gate, tri_left, tri_send, tri_right, lf, rf, part, ss, rs, ls,
):
    loads = {
        name: pltpu.make_async_copy(src, dst, ls.at[n])
        for n, (name, src, dst) in enumerate(
            (
                ("align", align_hbm, align_ref),
                ("wl", wl_hbm, wl_ref),
                ("wr", wr_hbm, wr_ref),
                ("amask", amask_hbm, amask_ref),
                ("oproj", oproj_hbm, oproj_ref),
                ("rmask", rmask_hbm, rmask_ref),
                ("pair", pair_hbm, pair_ref),
                ("tproj", tproj_hbm, tproj_ref),
                ("tgate", tgate_hbm, tgate_ref),
                ("tout", tout_hbm, tout_ref),
                ("tin", tin_hbm, tin_ref),
                ("trans", trans_hbm, trans_ref),
            )
        )
    }
    r, q = lax.axis_index("row"), lax.axis_index("col")
    z, x = r // 4, lax.rem(r, 4)
    zl, y, core = q // 8, lax.rem(q // 2, 4), lax.rem(q, 2)
    same = r == q

    def row_of(zz, xx):
        return lax.rem(zz + 4, 4) * 4 + lax.rem(xx + 4, 4)

    def col_of(ll, yy, cc):
        return (ll * 4 + lax.rem(yy + 4, 4)) * 2 + cc

    zp, zm = (row_of(z + 1, x), q), (row_of(z - 1, x), q)
    xp, xm = (row_of(z, x + 1), q), (row_of(z, x - 1), q)
    yp, ym = (r, col_of(zl, y + 1, core)), (r, col_of(zl, y - 1, core))
    zlo = (r, col_of(1 - zl, y, core))
    twin = (r, col_of(zl, y, 1 - core))

    barrier = pltpu.get_barrier_semaphore()
    def greet(t, carry):
        @pl.when(jnp.logical_not(same & (t == z)))
        def _():
            pl.semaphore_signal(
                barrier, inc=1, device_id=(t * 4 + lax.rem(q, 4), r), device_id_type=MESH
            )

        return carry

    for t in range(4):
        greet(t, 0)

    def greet_tri(t, carry):
        @pl.when(jnp.logical_not(same & (t * 4 + x == q)))
        def _():
            pl.semaphore_signal(barrier, inc=1, device_id=(q, t * 4 + x), device_id_type=MESH)

        return carry

    for t in range(4):
        greet_tri(t, 0)
    for device in (zp, zm, xp, xm, yp, ym, zlo, twin):
        pl.semaphore_signal(barrier, inc=1, device_id=device, device_id_type=MESH)

    for load in loads.values():
        load.start()

    loads["align"].wait()

    def norm_chunk(t, carry):
        rows = pl.ds(pl.multiple_of(t * 96, 96), 96)
        v = norm(align_ref[rows, :].astype(F32))
        xs[0, rows, :] = v[:, :128]
        xs[1, rows, :] = v[:, 128:]
        return carry

    lax.fori_loop(0, 8, norm_chunk, 0)

    lane = lax.broadcasted_iota(I32, (256, 128), 1)
    spread = (
        lax.rem(lax.broadcasted_iota(I32, (32, 128), 1), 32)
        == lax.broadcasted_iota(I32, (32, 128), 0)
    ).astype(F32).astype(BF16)
    loads["wl"].wait()
    loads["wr"].wait()
    for side, w_ref in enumerate((wl_ref, wr_ref)):
        w = dot(w_ref[...].astype(F32).T.astype(BF16), spread)
        for u in range(4):
            own = (lane >= 32 * u) & (lane < 32 * u + 32)
            wbd[256 * u : 256 * u + 256, 128 * side : 128 * side + 128] = jnp.where(
                own, w, 0.0
            ).astype(BF16)

    lam = lax.broadcasted_iota(I32, (1, 768), 1)
    by24 = (lam * 2731) // 65536
    target = (lam - by24 * 24) * 32 + by24

    def perm_chunk(t, carry):
        start = pl.multiple_of(t * 64, 64)
        rows = lax.broadcasted_iota(I32, (64, 768), 0) + start
        perm[pl.ds(start, 64), :] = (rows == target).astype(F32).astype(BF16)
        return carry

    lax.fori_loop(0, 12, perm_chunk, 0)

    loads["amask"].wait()
    amask = amask_ref[...].astype(F32).T.astype(BF16)
    row24 = lax.broadcasted_iota(I32, (24, 768), 0) * 32
    lane24 = lax.broadcasted_iota(I32, (24, 768), 1)
    expand = ((lane24 >= row24) & (lane24 < row24 + 32)).astype(F32).astype(BF16)
    mask_wide = dot(amask, expand)
    mask_lanes = dot(
        amask,
        (
            lax.broadcasted_iota(I32, (24, 128), 0) == lax.broadcasted_iota(I32, (24, 128), 1)
        ).astype(F32).astype(BF16),
    ).astype(BF16)
    own_rows = pl.ds(pl.multiple_of((x * 4 + z) * 32, 32), 32)
    for g in range(6):
        four = jnp.concatenate(
            [
                xs[half, pl.ds(4 * g + u, 32, stride=24), :].astype(BF16)
                for u in range(4)
                for half in range(2)
            ],
            axis=1,
        )
        both = dot(four, wbd[...])
        m = mask_wide[:, 128 * g : 128 * g + 128]
        lnat[:, 128 * g : 128 * g + 128] = (both[:, :128] * m).astype(BF16)
        right = (both[:, 128:] * m).astype(BF16)
        right_all[own_rows, 128 * g : 128 * g + 128] = right
    left = dot(lnat[...], perm[...]).astype(BF16)
    right_all[own_rows, 768:896] = mask_lanes
    for g in range(6):
        left_send[g // 2, g % 2] = left[:, 128 * g : 128 * g + 128]
    left_send[3, 0] = mask_lanes
    left_send[3, 1] = jnp.zeros((32, 128), BF16)

    def remote(src, dst, send, recv, device):
        return pltpu.make_async_remote_copy(
            src_ref=src, dst_ref=dst, send_sem=ss.at[send], recv_sem=rs.at[recv],
            device_id=device, device_id_type=MESH,
        )

    def send(ref, k, device):
        remote(ref, ref, k, k, device).start()

    def wait_recv(ref, k):
        remote(ref, ref, k, k, twin).wait_recv()

    def wait_send(ref, k):
        remote(ref, ref, k, k, twin).wait_send()

    class Ring:
        def __init__(self, slot, half, at, plus, minus, k):
            self.slot, self.half, self.at = slot, half, at
            self.plus, self.minus, self.k = plus, minus, k

        def pos(self, d):
            return lax.rem(self.at + d + 4, 4)

        def start(self):
            send(self.slot(self.at), self.k, self.plus)
            send(self.slot(self.at), self.k + 1, self.minus)

        def from_minus(self):
            wait_recv(self.slot(self.pos(-1)), self.k)
            send(self.half(self.pos(-1), 0), self.k + 2, self.plus)

        def from_plus(self):
            wait_recv(self.slot(self.pos(1)), self.k + 1)
            send(self.half(self.pos(1), 1), self.k + 3, self.minus)

        def finish(self):
            wait_recv(self.half(self.pos(2), 0), self.k + 2)
            wait_recv(self.half(self.pos(2), 1), self.k + 3)

        def drain(self):
            wait_send(self.slot(self.at), self.k)
            wait_send(self.slot(self.at), self.k + 1)
            wait_send(self.half(self.pos(-1), 0), self.k + 2)
            wait_send(self.half(self.pos(1), 1), self.k + 3)

    class Columns:
        def __init__(self, ref, half_rows, k):
            self.ref, self.k = ref, k

            def slot(ll):
                return lambda yy: ref.at[col_of(ll, yy, core)]

            def half(ll):
                return lambda yy, h: ref.at[
                    col_of(ll, yy, core), pl.ds(h * half_rows, half_rows)
                ]

            self.rings = [
                Ring(slot(ll), half(ll), y, yp, ym, k + 1 + 4 * e)
                for e, ll in enumerate((zl, 1 - zl))
            ]
            self.passed = []

        def to_twin(self, ll, yy):
            n = len(self.passed)
            at = lax.rem(yy + 4, 4)
            self.passed.append((ll, at))
            send(self.ref.at[col_of(ll, at, core)], self.k + 9 + n, twin)

        def start(self):
            send(self.ref.at[q], self.k, zlo)
            self.rings[0].start()
            self.to_twin(zl, y)

        def other_half(self):
            wait_recv(self.ref.at[col_of(1 - zl, y, core)], self.k)
            self.rings[1].start()
            self.to_twin(1 - zl, y)

        def from_minus(self, e):
            self.rings[e].from_minus()
            self.to_twin((zl, 1 - zl)[e], y - 1)

        def from_plus(self, e):
            self.rings[e].from_plus()
            self.to_twin((zl, 1 - zl)[e], y + 1)

        def finish(self, e):
            self.rings[e].finish()
            self.to_twin((zl, 1 - zl)[e], y + 2)

        def finish_twin(self):
            for n, (ll, at) in enumerate(self.passed):
                wait_recv(self.ref.at[col_of(ll, at, 1 - core)], self.k + 9 + n)

        def drain(self):
            wait_send(self.ref.at[q], self.k)
            for ring in self.rings:
                ring.drain()
            for n, (ll, at) in enumerate(self.passed):
                wait_send(self.ref.at[col_of(ll, at, core)], self.k + 9 + n)

    class Rows:
        def __init__(self, block, half, k):
            self.zring = Ring(
                lambda zz: block(zz, x), lambda zz, h: half(zz, x, h), z, zp, zm, k
            )

            def slot(zz):
                return lambda xx: block(zz, xx)

            def part(zz):
                return lambda xx, h: half(zz, xx, h)

            self.order = [z, lax.rem(z + 3, 4), lax.rem(z + 1, 4), lax.rem(z + 2, 4)]
            self.xrings = [
                Ring(slot(zz), part(zz), x, xp, xm, k + 4 + 4 * e)
                for e, zz in enumerate(self.order)
            ]

        def start(self):
            self.zring.start()
            self.xrings[0].start()

        def z_neighbours(self):
            self.zring.from_minus()
            self.xrings[1].start()
            self.zring.from_plus()
            self.xrings[2].start()

        def z_far(self):
            self.zring.finish()
            self.xrings[3].start()

        def x_neighbours(self, e):
            self.xrings[e].from_minus()
            self.xrings[e].from_plus()

        def x_far(self, e):
            self.xrings[e].finish()

        def drain(self):
            self.zring.drain()
            for ring in self.xrings:
                ring.drain()

    def right_rows(zz, xx, h, count):
        return pl.ds(pl.multiple_of((xx * 4 + zz) * 32 + 16 * h, 16), count)

    right_rows_gather = Rows(
        lambda zz, xx: right_all.at[right_rows(zz, xx, 0, 32)],
        lambda zz, xx, h: right_all.at[right_rows(zz, xx, h, 16)],
        RIGHT_GATHER,
    )
    left_columns = Columns(left_all, 2, LEFT_GATHER)

    def zero_chunk(t, carry):
        bd[pl.ds(pl.multiple_of(t * 64, 64), 64), :] = jnp.zeros((64, 256), BF16)
        part[pl.ds(pl.multiple_of(t * 144, 144), 144), :] = jnp.zeros((144, 128), F32)
        return carry

    lax.fori_loop(0, 32, zero_chunk, 0)
    loads["oproj"].wait()

    def fill_chunk(t, carry):
        block = oproj_ref[pl.ds(pl.multiple_of(t * 32, 32), 32), :]
        for u in range(2):
            bd[pl.ds(pl.multiple_of(t * 64 + 32 * u, 32), 32), 128 * u : 128 * u + 128] = block
        return carry

    lax.fori_loop(0, 32, fill_chunk, 0)
    loads["rmask"].wait()
    mask_k = jnp.zeros((24, 128), F32)
    sub = lax.broadcasted_iota(I32, (24, 128), 0)
    for k in range(24):
        mask_k = jnp.where(sub == k, rmask_ref[q * 24 + k].astype(F32), mask_k)
    for i in range(24):
        pmask[24 * i : 24 * i + 24, :] = mask_k * rmask_ref[r * 24 + i].astype(F32)
    for name in ("pair", "tproj", "tgate", "tout", "tin", "trans"):
        loads[name].wait()

    pl.semaphore_wait(barrier, 16 - 2 * same.astype(I32))

    def scatter(t, carry):
        is_self = same & (t == z)
        p = t * 4 + x

        @pl.when(jnp.logical_not(is_self))
        def _():
            remote(
                left_send.at[t], left_all.at[p, z], LEFT_SCATTER + t, LEFT_SCATTER + z, (q, p)
            ).start()

        @pl.when(is_self)
        def _():
            left_all[p, z] = left_send[t]

        return carry

    lax.fori_loop(0, 4, scatter, 0)
    right_rows_gather.start()

    def scatter_arrived(t, carry):
        @pl.when(jnp.logical_not(same & (t == z)))
        def _():
            piece = left_all.at[q, t]
            remote(piece, piece, LEFT_SCATTER + t, LEFT_SCATTER + t, twin).wait_recv()

        return carry

    lax.fori_loop(0, 4, scatter_arrived, 0)
    left_columns.start()
    right_rows_gather.z_neighbours()
    left_columns.other_half()
    left_columns.from_minus(0)
    left_columns.from_plus(0)
    right_rows_gather.x_neighbours(0)
    right_rows_gather.z_far()
    left_columns.from_minus(1)
    left_columns.from_plus(1)
    right_rows_gather.x_neighbours(1)
    right_rows_gather.x_neighbours(2)
    left_columns.finish(0)
    right_rows_gather.x_neighbours(3)
    left_columns.finish(1)

    def turn(m):
        lanes = pl.ds(pl.multiple_of(m * 128, 128), 128)
        for g in range(6):
            left_t[128 * g : 128 * g + 128, lanes] = (
                left_all[4 * (g // 2) + m, :, g % 2].reshape(128, 128).T
            )

    turn(core)
    turn(core + 2)
    left_columns.finish_twin()
    turn(1 - core)
    turn(3 - core)
    for e in range(4):
        right_rows_gather.x_far(e)

    counts = sum(
        dot(
            left_all[12 + m, :, 0].reshape(128, 128).T,
            right_all[128 * m : 128 * m + 128, 768:896],
        )
        for m in range(4)
    )
    counts = jnp.maximum(counts[:24], 1.0)
    low = lax.broadcasted_iota(I32, (24, 128), 1) < 64
    for g in range(3):
        outer = dot(left_t[...], right_all[:, 256 * g : 256 * g + 256])
        for u in range(2):
            tile = outer[:, 128 * u : 128 * u + 128]
            turned = pltpu.roll(tile, 64, 1)
            at = 32 * (2 * g + u)
            for c in range(0, 32, 2):
                even, odd = slice(24 * c, 24 * c + 24), slice(24 * c + 24, 24 * c + 48)
                lanes = slice(64 * c, 64 * c + 128)
                lhs2[at : at + 24, lanes] = jnp.where(low, tile[even], turned[odd]).astype(BF16)
                lhs2[192 + at : 192 + at + 24, lanes] = jnp.where(
                    low, turned[even], tile[odd]
                ).astype(BF16)
    both_proj = dot(lhs2[...], bd[...])
    for n in range(2):
        proj = both_proj[192 * n : 192 * n + 192]
        for g in range(6):
            for u in range(2):
                j = 4 * g + 2 * n + u
                ptile[24 * j : 24 * j + 24, :] = (
                    proj[32 * g : 32 * g + 24, 128 * u : 128 * u + 128] / counts[:, j : j + 1]
                )
    for i in range(0, 24, 2):
        rows = slice(24 * i, 24 * i + 48)
        tiles = [ptile[pl.ds(i + v, 24, stride=24), :] for v in range(2)]
        rounded = (pair_ref[rows, :].astype(F32) + jnp.concatenate(tiles, axis=0)).astype(BF16)
        rounded = rounded.astype(F32)
        first[rows, :] = rounded
        normed[rows, :] = norm(rounded).astype(BF16)

    tri_columns = Columns(tri_left, 288, TRI_LEFT)

    def chunk(n):
        return Rows(
            lambda zz, xx: tri_right.at[xx, zz, pl.ds(2 * n, 2)],
            lambda zz, xx, h: tri_right.at[xx, zz, pl.ds(2 * n + h, 1)],
            TRI_RIGHT + 20 * n,
        )

    rows0, rows1 = chunk(0), chunk(1)
    holder, place = lax.rem(q, 4), q // 4

    def tri_scatter(t, carry):
        is_self = same & (t == z)
        piece = pl.ds(t * 144, 144)

        @pl.when(jnp.logical_not(is_self))
        def _():
            remote(
                tri_send.at[piece], tri_right.at[holder, t, place], TRI_SCATTER + t,
                TRI_SCATTER + place, (t * 4 + holder, r),
            ).start()

        @pl.when(is_self)
        def _():
            tri_right[holder, t, place] = tri_send[piece, :]

        return carry

    for t in range(3):
        rows = slice(192 * t, 192 * t + 192)
        p = dot(normed[rows, :], tproj_ref[:, 256:])
        tri_send[rows, :] = (jax.nn.sigmoid(p[:, :128]) * p[:, 128:] * pmask[rows, :]).astype(BF16)
    for t in range(4):
        tri_scatter(t, 0)
    for t in range(3):
        rows = slice(192 * t, 192 * t + 192)
        p = dot(normed[rows, :], tproj_ref[:, :256])
        tri_left[q, rows, :] = (
            jax.nn.sigmoid(p[:, :128]) * p[:, 128:] * pmask[rows, :]
        ).astype(BF16)
    tri_columns.start()

    def tri_arrived(t, carry):
        @pl.when(jnp.logical_not(same & (t == place)))
        def _():
            piece = tri_right.at[x, z, t]
            remote(piece, piece, TRI_SCATTER + t, TRI_SCATTER + t, twin).wait_recv()

        return carry

    lax.fori_loop(0, 4, tri_arrived, 0)
    rows0.start()
    rows1.start()
    tri_columns.other_half()

    gate[...] = jax.nn.sigmoid(dot(normed[...], tgate_ref[...]))

    def widen_left(xx):
        def widen(t, carry):
            b, rows = t // 4, pl.ds(pl.multiple_of(lax.rem(t, 4) * 144, 144), 144)
            lf[xx, b, rows, :] = tri_left[b * 4 + xx, rows, :].astype(F32)
            return carry

        lax.fori_loop(0, 16, widen, 0)

    def accumulate(xx, zz, first_block=0, last_block=4):
        def widen(t, carry):
            rf[t] = tri_right[xx, zz, t].astype(F32)
            return carry

        lax.fori_loop(first_block, last_block, widen, 0)

        def block(t, carry):
            def at(u, v):
                return pl.ds(pl.multiple_of(((t * 4 + u) * 24 + zz * 6 + v) * 8, 8), 8)

            acc = [[part[at(u, v), :] for v in range(6)] for u in range(4)]
            for b in range(first_block, last_block):
                for k in range(3):
                    left = [
                        lf[xx, b, pl.ds(pl.multiple_of((t * 4 + u) * 24 + 8 * k, 8), 8), :]
                        for u in range(4)
                    ]
                    right = [rf[b, 24 * v + 8 * k : 24 * v + 8 * k + 8, :] for v in range(6)]
                    for u in range(4):
                        for v in range(6):
                            acc[u][v] = acc[u][v] + left[u] * right[v]
            for u in range(4):
                for v in range(6):
                    part[at(u, v), :] = acc[u][v]
            return carry

        lax.fori_loop(0, 6, block, 0)

    def xat(d):
        return lax.rem(x + d + 4, 4)

    tri_columns.from_minus(0)
    tri_columns.from_plus(0)
    rows0.z_neighbours()
    rows0.x_neighbours(0)
    tri_columns.from_minus(1)
    tri_columns.from_plus(1)
    rows1.z_neighbours()
    rows1.x_neighbours(0)
    tri_columns.finish(0)
    rows0.z_far()
    tri_columns.finish(1)
    rows0.x_neighbours(1)
    rows0.x_neighbours(2)
    tri_columns.finish_twin()
    order = rows0.order
    widen_left(x)
    accumulate(x, order[0])
    rows1.z_far()
    rows1.x_neighbours(1)
    accumulate(x, order[1])
    rows1.x_neighbours(2)
    accumulate(x, order[2])
    accumulate(x, order[3])
    for d in (-1, 1):
        widen_left(xat(d))
    accumulate(xat(-1), order[0])
    rows0.x_neighbours(3)
    accumulate(xat(1), order[0])
    accumulate(xat(-1), order[1])
    rows1.x_neighbours(3)
    accumulate(xat(1), order[1])
    accumulate(xat(-1), order[2])
    accumulate(xat(1), order[2])
    widen_left(xat(2))
    for e in range(3):
        rows0.x_far(e)
        rows1.x_far(e)
        accumulate(xat(2), order[e])
    accumulate(xat(-1), order[3])
    accumulate(xat(1), order[3])
    rows0.x_far(3)
    accumulate(xat(2), order[3], 0, 2)
    rows1.x_far(3)
    accumulate(xat(2), order[3], 2, 4)

    for t in range(1):
        rows = slice(576 * t, 576 * t + 576)
        summed = part[pl.ds(2304 * t, 576, stride=8), :]
        for k in range(1, 8):
            summed = summed + part[pl.ds(2304 * t + k, 576, stride=8), :]
        normed_sum = norm(summed).astype(BF16)
        second = (first[rows, :] + gate[rows, :] * dot(normed_sum, tout_ref[...])).astype(BF16)
        second = second.astype(F32)
        hidden = jnp.maximum(dot(norm(second).astype(BF16), tin_ref[...]), 0.0).astype(BF16)
        out_ref[rows, :] = (second + dot(hidden, trans_ref[...])).astype(BF16)

    def scatter_left(t, carry):
        @pl.when(jnp.logical_not(same & (t == z)))
        def _():
            remote(
                left_send.at[t], left_send.at[t], LEFT_SCATTER + t, LEFT_SCATTER + t, twin
            ).wait_send()

        return carry

    lax.fori_loop(0, 4, scatter_left, 0)

    def tri_left_here(t, carry):
        @pl.when(jnp.logical_not(same & (t == z)))
        def _():
            piece = tri_send.at[pl.ds(pl.multiple_of(t * 144, 144), 144)]
            remote(piece, piece, TRI_SCATTER + t, TRI_SCATTER + t, twin).wait_send()

        return carry

    lax.fori_loop(0, 4, tri_left_here, 0)
    left_columns.drain()
    right_rows_gather.drain()
    tri_columns.drain()
    rows0.drain()
    rows1.drain()


def shards(alignment, alignment_mask, residue_mask, pair_features, *weights):
    vmem = pl.BlockSpec(memory_space=pltpu.VMEM)
    hbm = pl.BlockSpec(memory_space=pltpu.HBM)
    out = pl.pallas_call(
        kernel,
        out_shape=jax.ShapeDtypeStruct((576, 128), BF16),
        in_specs=[hbm] * 12,
        out_specs=vmem,
        scratch_shapes=[
            pltpu.VMEM((768, 256), BF16),
            pltpu.VMEM((24, 32), I32),
            pltpu.SMEM((384,), I32),
            pltpu.VMEM((576, 128), BF16),
            pltpu.VMEM((32, 256), BF16),
            pltpu.VMEM((32, 256), BF16),
            pltpu.VMEM((1024, 128), BF16),
            pltpu.VMEM((128, 512), BF16),
            pltpu.VMEM((128, 128), BF16),
            pltpu.VMEM((128, 128), BF16),
            pltpu.VMEM((128, 512), BF16),
            pltpu.VMEM((512, 128), BF16),
            pltpu.VMEM((2, 768, 128), F32),
            pltpu.VMEM((1024, 256), BF16),
            pltpu.VMEM((768, 768), BF16),
            pltpu.VMEM((2048, 256), BF16),
            pltpu.VMEM((32, 768), BF16),
            pltpu.VMEM((4, 2, 32, 128), BF16),
            pltpu.VMEM((16, 4, 2, 32, 128), BF16),
            pltpu.VMEM((512, 896), BF16),
            pltpu.VMEM((768, 512), BF16),
            pltpu.VMEM((384, 2048), BF16),
            pltpu.VMEM((576, 128), F32),
            pltpu.VMEM((576, 128), F32),
            pltpu.VMEM((576, 128), BF16),
            pltpu.VMEM((576, 128), F32),
            pltpu.VMEM((576, 128), F32),
            pltpu.VMEM((16, 576, 128), BF16),
            pltpu.VMEM((576, 128), BF16),
            pltpu.VMEM((4, 4, 4, 144, 128), BF16),
            pltpu.VMEM((4, 4, 576, 128), F32),
            pltpu.VMEM((4, 144, 128), F32),
            pltpu.VMEM((4608, 128), F32),
            pltpu.SemaphoreType.DMA((TRANSFERS,)),
            pltpu.SemaphoreType.DMA((TRANSFERS,)),
            pltpu.SemaphoreType.DMA((12,)),
        ],
        compiler_params=pltpu.CompilerParams(
            collective_id=0, has_side_effects=True, vmem_limit_bytes=60 * 1024 * 1024
        ),
        cost_estimate=pl.CostEstimate(
            flops=1_500_000_000, bytes_accessed=2_000_000, transcendentals=400_000
        ),
    )(
        alignment.reshape(768, 256), alignment_mask.T, residue_mask, pair_features.reshape(576, 128),
        weights[0].T, weights[1].T, *weights[2:],
    )
    return out.reshape(24, 24, 128)


def solution(mesh):
    placed = (P("row", "col", None), P("row", "col"), P(), P("row", "col", None)) + (P(),) * 8
    return jax.shard_map(
        shards, mesh=mesh, in_specs=placed, out_specs=P("row", "col", None), check_vma=False
    )
```

```python
import jax
import jax.numpy as jnp
from jax import lax
from jax.experimental import pallas as pl
from jax.experimental.pallas import tpu as pltpu
from jax.sharding import PartitionSpec as P

EPSILON = 1e-05
MESH = pl.DeviceIdType.MESH
F32 = jnp.float32
BF16 = jnp.bfloat16
I32 = jnp.int32

LEFT_SCATTER = 0
LEFT_GATHER = 4
RIGHT_GATHER = 21
TRI_SCATTER = 41
TRI_LEFT = 45
TRI_RIGHT = 62
TRANSFERS = 102


def norm(v):
    mean = jnp.mean(v, axis=-1, keepdims=True)
    centered = v - mean
    variance = jnp.mean(centered * centered, axis=-1, keepdims=True)
    return centered * lax.rsqrt(variance + EPSILON)


def dot(a, b):
    return jnp.dot(a, b, preferred_element_type=F32)


def kernel(
    align_hbm, amask_hbm, rmask_hbm, pair_hbm, wl_hbm, wr_hbm, oproj_hbm, tproj_hbm, tgate_hbm,
    tout_hbm, tin_hbm, trans_hbm, out_ref,
    align_ref, amask_ref, rmask_ref, pair_ref, wl_ref, wr_ref, oproj_ref, tproj_ref, tgate_ref,
    tout_ref, tin_ref, trans_ref,
    xs, wbd, perm, bd, lnat, left_send, left_all, right_all, left_t, lhs2, ptile, first, normed,
    pmask, gate, tri_left, tri_send, tri_right, lf, rf, part, ss, rs, ls,
):
    loads = {
        name: pltpu.make_async_copy(src, dst, ls.at[n])
        for n, (name, src, dst) in enumerate(
            (
                ("align", align_hbm, align_ref),
                ("wl", wl_hbm, wl_ref),
                ("wr", wr_hbm, wr_ref),
                ("amask", amask_hbm, amask_ref),
                ("oproj", oproj_hbm, oproj_ref),
                ("rmask", rmask_hbm, rmask_ref),
                ("pair", pair_hbm, pair_ref),
                ("tproj", tproj_hbm, tproj_ref),
                ("tgate", tgate_hbm, tgate_ref),
                ("tout", tout_hbm, tout_ref),
                ("tin", tin_hbm, tin_ref),
                ("trans", trans_hbm, trans_ref),
            )
        )
    }
    r, q = lax.axis_index("row"), lax.axis_index("col")
    z, x = r // 4, lax.rem(r, 4)
    zl, y, core = q // 8, lax.rem(q // 2, 4), lax.rem(q, 2)
    same = r == q

    def row_of(zz, xx):
        return lax.rem(zz + 4, 4) * 4 + lax.rem(xx + 4, 4)

    def col_of(ll, yy, cc):
        return (ll * 4 + lax.rem(yy + 4, 4)) * 2 + cc

    zp, zm = (row_of(z + 1, x), q), (row_of(z - 1, x), q)
    xp, xm = (row_of(z, x + 1), q), (row_of(z, x - 1), q)
    yp, ym = (r, col_of(zl, y + 1, core)), (r, col_of(zl, y - 1, core))
    zlo = (r, col_of(1 - zl, y, core))
    twin = (r, col_of(zl, y, 1 - core))

    barrier = pltpu.get_barrier_semaphore()
    def greet(t, carry):
        @pl.when(jnp.logical_not(same & (t == z)))
        def _():
            pl.semaphore_signal(
                barrier, inc=1, device_id=(t * 4 + lax.rem(q, 4), r), device_id_type=MESH
            )

        return carry

    for t in range(4):
        greet(t, 0)

    def greet_tri(t, carry):
        @pl.when(jnp.logical_not(same & (t * 4 + x == q)))
        def _():
            pl.semaphore_signal(barrier, inc=1, device_id=(q, t * 4 + x), device_id_type=MESH)

        return carry

    for t in range(4):
        greet_tri(t, 0)
    for device in (zp, zm, xp, xm, yp, ym, zlo, twin):
        pl.semaphore_signal(barrier, inc=1, device_id=device, device_id_type=MESH)

    for load in loads.values():
        load.start()

    loads["align"].wait()

    def norm_chunk(t, carry):
        rows = pl.ds(pl.multiple_of(t * 96, 96), 96)
        v = norm(align_ref[rows, :].astype(F32))
        xs[0, rows, :] = v[:, :128]
        xs[1, rows, :] = v[:, 128:]
        return carry

    lax.fori_loop(0, 8, norm_chunk, 0)

    lane = lax.broadcasted_iota(I32, (256, 128), 1)
    spread = (
        lax.rem(lax.broadcasted_iota(I32, (32, 128), 1), 32)
        == lax.broadcasted_iota(I32, (32, 128), 0)
    ).astype(F32).astype(BF16)
    loads["wl"].wait()
    loads["wr"].wait()
    for side, w_ref in enumerate((wl_ref, wr_ref)):
        w = dot(w_ref[...].astype(F32).T.astype(BF16), spread)
        for u in range(4):
            own = (lane >= 32 * u) & (lane < 32 * u + 32)
            wbd[256 * u : 256 * u + 256, 128 * side : 128 * side + 128] = jnp.where(
                own, w, 0.0
            ).astype(BF16)

    lam = lax.broadcasted_iota(I32, (1, 768), 1)
    by24 = (lam * 2731) // 65536
    target = (lam - by24 * 24) * 32 + by24

    def perm_chunk(t, carry):
        start = pl.multiple_of(t * 64, 64)
        rows = lax.broadcasted_iota(I32, (64, 768), 0) + start
        perm[pl.ds(start, 64), :] = (rows == target).astype(F32).astype(BF16)
        return carry

    lax.fori_loop(0, 12, perm_chunk, 0)

    loads["amask"].wait()
    amask = amask_ref[...].astype(F32).T.astype(BF16)
    row24 = lax.broadcasted_iota(I32, (24, 768), 0) * 32
    lane24 = lax.broadcasted_iota(I32, (24, 768), 1)
    expand = ((lane24 >= row24) & (lane24 < row24 + 32)).astype(F32).astype(BF16)
    mask_wide = dot(amask, expand)
    mask_lanes = dot(
        amask,
        (
            lax.broadcasted_iota(I32, (24, 128), 0) == lax.broadcasted_iota(I32, (24, 128), 1)
        ).astype(F32).astype(BF16),
    ).astype(BF16)
    own_rows = pl.ds(pl.multiple_of((x * 4 + z) * 32, 32), 32)
    for g in range(6):
        four = jnp.concatenate(
            [
                xs[half, pl.ds(4 * g + u, 32, stride=24), :].astype(BF16)
                for u in range(4)
                for half in range(2)
            ],
            axis=1,
        )
        both = dot(four, wbd[...])
        m = mask_wide[:, 128 * g : 128 * g + 128]
        lnat[:, 128 * g : 128 * g + 128] = (both[:, :128] * m).astype(BF16)
        right = (both[:, 128:] * m).astype(BF16)
        right_all[own_rows, 128 * g : 128 * g + 128] = right
    left = dot(lnat[...], perm[...]).astype(BF16)
    right_all[own_rows, 768:896] = mask_lanes
    for g in range(6):
        left_send[g // 2, g % 2] = left[:, 128 * g : 128 * g + 128]
    left_send[3, 0] = mask_lanes
    left_send[3, 1] = jnp.zeros((32, 128), BF16)

    def remote(src, dst, send, recv, device):
        return pltpu.make_async_remote_copy(
            src_ref=src, dst_ref=dst, send_sem=ss.at[send], recv_sem=rs.at[recv],
            device_id=device, device_id_type=MESH,
        )

    def send(ref, k, device):
        remote(ref, ref, k, k, device).start()

    def wait_recv(ref, k):
        remote(ref, ref, k, k, twin).wait_recv()

    def wait_send(ref, k):
        remote(ref, ref, k, k, twin).wait_send()

    class Ring:
        def __init__(self, slot, half, at, plus, minus, k):
            self.slot, self.half, self.at = slot, half, at
            self.plus, self.minus, self.k = plus, minus, k

        def pos(self, d):
            return lax.rem(self.at + d + 4, 4)

        def start(self):
            send(self.slot(self.at), self.k, self.plus)
            send(self.slot(self.at), self.k + 1, self.minus)

        def from_minus(self):
            wait_recv(self.slot(self.pos(-1)), self.k)
            send(self.half(self.pos(-1), 0), self.k + 2, self.plus)

        def from_plus(self):
            wait_recv(self.slot(self.pos(1)), self.k + 1)
            send(self.half(self.pos(1), 1), self.k + 3, self.minus)

        def finish(self):
            wait_recv(self.half(self.pos(2), 0), self.k + 2)
            wait_recv(self.half(self.pos(2), 1), self.k + 3)

        def drain(self):
            wait_send(self.slot(self.at), self.k)
            wait_send(self.slot(self.at), self.k + 1)
            wait_send(self.half(self.pos(-1), 0), self.k + 2)
            wait_send(self.half(self.pos(1), 1), self.k + 3)

    class Columns:
        def __init__(self, ref, half_rows, k):
            self.ref, self.k = ref, k

            def slot(ll):
                return lambda yy: ref.at[col_of(ll, yy, core)]

            def half(ll):
                return lambda yy, h: ref.at[
                    col_of(ll, yy, core), pl.ds(h * half_rows, half_rows)
                ]

            self.rings = [
                Ring(slot(ll), half(ll), y, yp, ym, k + 1 + 4 * e)
                for e, ll in enumerate((zl, 1 - zl))
            ]
            self.passed = []

        def to_twin(self, ll, yy):
            n = len(self.passed)
            at = lax.rem(yy + 4, 4)
            self.passed.append((ll, at))
            send(self.ref.at[col_of(ll, at, core)], self.k + 9 + n, twin)

        def start(self):
            send(self.ref.at[q], self.k, zlo)
            self.rings[0].start()
            self.to_twin(zl, y)

        def other_half(self):
            wait_recv(self.ref.at[col_of(1 - zl, y, core)], self.k)
            self.rings[1].start()
            self.to_twin(1 - zl, y)

        def from_minus(self, e):
            self.rings[e].from_minus()
            self.to_twin((zl, 1 - zl)[e], y - 1)

        def from_plus(self, e):
            self.rings[e].from_plus()
            self.to_twin((zl, 1 - zl)[e], y + 1)

        def finish(self, e):
            self.rings[e].finish()
            self.to_twin((zl, 1 - zl)[e], y + 2)

        def finish_twin(self):
            for n, (ll, at) in enumerate(self.passed):
                wait_recv(self.ref.at[col_of(ll, at, 1 - core)], self.k + 9 + n)

        def drain(self):
            wait_send(self.ref.at[q], self.k)
            for ring in self.rings:
                ring.drain()
            for n, (ll, at) in enumerate(self.passed):
                wait_send(self.ref.at[col_of(ll, at, core)], self.k + 9 + n)

    class Rows:
        def __init__(self, block, half, k):
            self.zring = Ring(
                lambda zz: block(zz, x), lambda zz, h: half(zz, x, h), z, zp, zm, k
            )

            def slot(zz):
                return lambda xx: block(zz, xx)

            def part(zz):
                return lambda xx, h: half(zz, xx, h)

            self.order = [z, lax.rem(z + 3, 4), lax.rem(z + 1, 4), lax.rem(z + 2, 4)]
            self.xrings = [
                Ring(slot(zz), part(zz), x, xp, xm, k + 4 + 4 * e)
                for e, zz in enumerate(self.order)
            ]

        def start(self):
            self.zring.start()
            self.xrings[0].start()

        def z_neighbours(self):
            self.zring.from_minus()
            self.xrings[1].start()
            self.zring.from_plus()
            self.xrings[2].start()

        def z_far(self):
            self.zring.finish()
            self.xrings[3].start()

        def x_neighbours(self, e):
            self.xrings[e].from_minus()
            self.xrings[e].from_plus()

        def x_far(self, e):
            self.xrings[e].finish()

        def drain(self):
            self.zring.drain()
            for ring in self.xrings:
                ring.drain()

    def right_rows(zz, xx, h, count):
        return pl.ds(pl.multiple_of((xx * 4 + zz) * 32 + 16 * h, 16), count)

    right_rows_gather = Rows(
        lambda zz, xx: right_all.at[right_rows(zz, xx, 0, 32)],
        lambda zz, xx, h: right_all.at[right_rows(zz, xx, h, 16)],
        RIGHT_GATHER,
    )
    left_columns = Columns(left_all, 2, LEFT_GATHER)

    def zero_chunk(t, carry):
        bd[pl.ds(pl.multiple_of(t * 64, 64), 64), :] = jnp.zeros((64, 256), BF16)
        part[pl.ds(pl.multiple_of(t * 144, 144), 144), :] = jnp.zeros((144, 128), F32)
        return carry

    lax.fori_loop(0, 32, zero_chunk, 0)
    loads["oproj"].wait()

    def fill_chunk(t, carry):
        block = oproj_ref[pl.ds(pl.multiple_of(t * 32, 32), 32), :]
        for u in range(2):
            bd[pl.ds(pl.multiple_of(t * 64 + 32 * u, 32), 32), 128 * u : 128 * u + 128] = block
        return carry

    lax.fori_loop(0, 32, fill_chunk, 0)
    loads["rmask"].wait()
    mask_k = jnp.zeros((24, 128), F32)
    sub = lax.broadcasted_iota(I32, (24, 128), 0)
    for k in range(24):
        mask_k = jnp.where(sub == k, rmask_ref[q * 24 + k].astype(F32), mask_k)
    for i in range(24):
        pmask[24 * i : 24 * i + 24, :] = mask_k * rmask_ref[r * 24 + i].astype(F32)
    for name in ("pair", "tproj", "tgate", "tout", "tin", "trans"):
        loads[name].wait()

    pl.semaphore_wait(barrier, 16 - 2 * same.astype(I32))

    def scatter(t, carry):
        is_self = same & (t == z)
        p = t * 4 + x

        @pl.when(jnp.logical_not(is_self))
        def _():
            remote(
                left_send.at[t], left_all.at[p, z], LEFT_SCATTER + t, LEFT_SCATTER + z, (q, p)
            ).start()

        @pl.when(is_self)
        def _():
            left_all[p, z] = left_send[t]

        return carry

    lax.fori_loop(0, 4, scatter, 0)
    right_rows_gather.start()

    def scatter_arrived(t, carry):
        @pl.when(jnp.logical_not(same & (t == z)))
        def _():
            piece = left_all.at[q, t]
            remote(piece, piece, LEFT_SCATTER + t, LEFT_SCATTER + t, twin).wait_recv()

        return carry

    lax.fori_loop(0, 4, scatter_arrived, 0)
    left_columns.start()
    left_columns.other_half()
    right_rows_gather.z_neighbours()
    left_columns.from_minus(0)
    left_columns.from_plus(0)
    right_rows_gather.x_neighbours(0)
    right_rows_gather.z_far()
    left_columns.from_minus(1)
    left_columns.from_plus(1)
    right_rows_gather.x_neighbours(1)
    right_rows_gather.x_neighbours(2)
    left_columns.finish(0)
    right_rows_gather.x_neighbours(3)
    left_columns.finish(1)

    def turn(m):
        lanes = pl.ds(pl.multiple_of(m * 128, 128), 128)
        for g in range(6):
            left_t[128 * g : 128 * g + 128, lanes] = (
                left_all[4 * (g // 2) + m, :, g % 2].reshape(128, 128).T
            )

    turn(core)
    turn(core + 2)
    left_columns.finish_twin()
    turn(1 - core)
    turn(3 - core)
    for e in range(4):
        right_rows_gather.x_far(e)

    counts = sum(
        dot(
            left_all[12 + m, :, 0].reshape(128, 128).T,
            right_all[128 * m : 128 * m + 128, 768:896],
        )
        for m in range(4)
    )
    counts = jnp.maximum(counts[:24], 1.0)
    low = lax.broadcasted_iota(I32, (24, 128), 1) < 64
    for g in range(3):
        outer = dot(left_t[...], right_all[:, 256 * g : 256 * g + 256])
        for u in range(2):
            tile = outer[:, 128 * u : 128 * u + 128]
            turned = pltpu.roll(tile, 64, 1)
            at = 32 * (2 * g + u)
            for c in range(0, 32, 2):
                even, odd = slice(24 * c, 24 * c + 24), slice(24 * c + 24, 24 * c + 48)
                lanes = slice(64 * c, 64 * c + 128)
                lhs2[at : at + 24, lanes] = jnp.where(low, tile[even], turned[odd]).astype(BF16)
                lhs2[192 + at : 192 + at + 24, lanes] = jnp.where(
                    low, turned[even], tile[odd]
                ).astype(BF16)
    both_proj = dot(lhs2[...], bd[...])
    for n in range(2):
        proj = both_proj[192 * n : 192 * n + 192]
        for g in range(6):
            for u in range(2):
                j = 4 * g + 2 * n + u
                ptile[24 * j : 24 * j + 24, :] = (
                    proj[32 * g : 32 * g + 24, 128 * u : 128 * u + 128] / counts[:, j : j + 1]
                )
    for i in range(0, 24, 2):
        rows = slice(24 * i, 24 * i + 48)
        tiles = [ptile[pl.ds(i + v, 24, stride=24), :] for v in range(2)]
        rounded = (pair_ref[rows, :].astype(F32) + jnp.concatenate(tiles, axis=0)).astype(BF16)
        rounded = rounded.astype(F32)
        first[rows, :] = rounded
        normed[rows, :] = norm(rounded).astype(BF16)

    tri_columns = Columns(tri_left, 288, TRI_LEFT)

    def chunk(n):
        return Rows(
            lambda zz, xx: tri_right.at[xx, zz, pl.ds(2 * n, 2)],
            lambda zz, xx, h: tri_right.at[xx, zz, pl.ds(2 * n + h, 1)],
            TRI_RIGHT + 20 * n,
        )

    rows0, rows1 = chunk(0), chunk(1)
    holder, place = lax.rem(q, 4), q // 4

    def tri_scatter(t, carry):
        is_self = same & (t == z)
        piece = pl.ds(t * 144, 144)

        @pl.when(jnp.logical_not(is_self))
        def _():
            remote(
                tri_send.at[piece], tri_right.at[holder, t, place], TRI_SCATTER + t,
                TRI_SCATTER + place, (t * 4 + holder, r),
            ).start()

        @pl.when(is_self)
        def _():
            tri_right[holder, t, place] = tri_send[piece, :]

        return carry

    for t in range(3):
        rows = slice(192 * t, 192 * t + 192)
        p = dot(normed[rows, :], tproj_ref[:, 256:])
        tri_send[rows, :] = (jax.nn.sigmoid(p[:, :128]) * p[:, 128:] * pmask[rows, :]).astype(BF16)
    for t in range(4):
        tri_scatter(t, 0)
    for t in range(3):
        rows = slice(192 * t, 192 * t + 192)
        p = dot(normed[rows, :], tproj_ref[:, :256])
        tri_left[q, rows, :] = (
            jax.nn.sigmoid(p[:, :128]) * p[:, 128:] * pmask[rows, :]
        ).astype(BF16)
    tri_columns.start()

    def tri_arrived(t, carry):
        @pl.when(jnp.logical_not(same & (t == place)))
        def _():
            piece = tri_right.at[x, z, t]
            remote(piece, piece, TRI_SCATTER + t, TRI_SCATTER + t, twin).wait_recv()

        return carry

    lax.fori_loop(0, 4, tri_arrived, 0)
    rows0.start()
    rows1.start()
    tri_columns.other_half()

    gate[...] = jax.nn.sigmoid(dot(normed[...], tgate_ref[...]))

    def widen_left(xx):
        def widen(t, carry):
            b, rows = t // 4, pl.ds(pl.multiple_of(lax.rem(t, 4) * 144, 144), 144)
            lf[xx, b, rows, :] = tri_left[b * 4 + xx, rows, :].astype(F32)
            return carry

        lax.fori_loop(0, 16, widen, 0)

    def accumulate(xx, zz, first_block=0, last_block=4):
        def widen(t, carry):
            rf[t] = tri_right[xx, zz, t].astype(F32)
            return carry

        lax.fori_loop(first_block, last_block, widen, 0)

        def block(t, carry):
            def at(u, v):
                return pl.ds(pl.multiple_of(((t * 4 + u) * 24 + zz * 6 + v) * 8, 8), 8)

            acc = [[part[at(u, v), :] for v in range(6)] for u in range(4)]
            for b in range(first_block, last_block):
                for k in range(3):
                    left = [
                        lf[xx, b, pl.ds(pl.multiple_of((t * 4 + u) * 24 + 8 * k, 8), 8), :]
                        for u in range(4)
                    ]
                    right = [rf[b, 24 * v + 8 * k : 24 * v + 8 * k + 8, :] for v in range(6)]
                    for u in range(4):
                        for v in range(6):
                            acc[u][v] = acc[u][v] + left[u] * right[v]
            for u in range(4):
                for v in range(6):
                    part[at(u, v), :] = acc[u][v]
            return carry

        lax.fori_loop(0, 6, block, 0)

    def xat(d):
        return lax.rem(x + d + 4, 4)

    tri_columns.from_minus(0)
    tri_columns.from_plus(0)
    rows0.z_neighbours()
    rows0.x_neighbours(0)
    tri_columns.from_minus(1)
    tri_columns.from_plus(1)
    rows1.z_neighbours()
    rows1.x_neighbours(0)
    tri_columns.finish(0)
    rows0.z_far()
    tri_columns.finish(1)
    rows0.x_neighbours(1)
    rows0.x_neighbours(2)
    tri_columns.finish_twin()
    order = rows0.order
    widen_left(x)
    accumulate(x, order[0])
    rows1.z_far()
    rows1.x_neighbours(1)
    accumulate(x, order[1])
    rows1.x_neighbours(2)
    accumulate(x, order[2])
    accumulate(x, order[3])
    for d in (-1, 1):
        widen_left(xat(d))
    accumulate(xat(-1), order[0])
    rows0.x_neighbours(3)
    accumulate(xat(1), order[0])
    accumulate(xat(-1), order[1])
    rows1.x_neighbours(3)
    accumulate(xat(1), order[1])
    accumulate(xat(-1), order[2])
    accumulate(xat(1), order[2])
    widen_left(xat(2))
    for e in range(3):
        rows0.x_far(e)
        rows1.x_far(e)
        accumulate(xat(2), order[e])
    accumulate(xat(-1), order[3])
    accumulate(xat(1), order[3])
    rows0.x_far(3)
    accumulate(xat(2), order[3], 0, 2)
    rows1.x_far(3)
    accumulate(xat(2), order[3], 2, 4)

    for t in range(1):
        rows = slice(576 * t, 576 * t + 576)
        summed = part[pl.ds(2304 * t, 576, stride=8), :]
        for k in range(1, 8):
            summed = summed + part[pl.ds(2304 * t + k, 576, stride=8), :]
        normed_sum = norm(summed).astype(BF16)
        second = (first[rows, :] + gate[rows, :] * dot(normed_sum, tout_ref[...])).astype(BF16)
        second = second.astype(F32)
        hidden = jnp.maximum(dot(norm(second).astype(BF16), tin_ref[...]), 0.0).astype(BF16)
        out_ref[rows, :] = (second + dot(hidden, trans_ref[...])).astype(BF16)

    def scatter_left(t, carry):
        @pl.when(jnp.logical_not(same & (t == z)))
        def _():
            remote(
                left_send.at[t], left_send.at[t], LEFT_SCATTER + t, LEFT_SCATTER + t, twin
            ).wait_send()

        return carry

    lax.fori_loop(0, 4, scatter_left, 0)

    def tri_left_here(t, carry):
        @pl.when(jnp.logical_not(same & (t == z)))
        def _():
            piece = tri_send.at[pl.ds(pl.multiple_of(t * 144, 144), 144)]
            remote(piece, piece, TRI_SCATTER + t, TRI_SCATTER + t, twin).wait_send()

        return carry

    lax.fori_loop(0, 4, tri_left_here, 0)
    left_columns.drain()
    right_rows_gather.drain()
    tri_columns.drain()
    rows0.drain()
    rows1.drain()


def shards(alignment, alignment_mask, residue_mask, pair_features, *weights):
    vmem = pl.BlockSpec(memory_space=pltpu.VMEM)
    hbm = pl.BlockSpec(memory_space=pltpu.HBM)
    out = pl.pallas_call(
        kernel,
        out_shape=jax.ShapeDtypeStruct((576, 128), BF16),
        in_specs=[hbm] * 12,
        out_specs=vmem,
        scratch_shapes=[
            pltpu.VMEM((768, 256), BF16),
            pltpu.VMEM((24, 32), I32),
            pltpu.SMEM((384,), I32),
            pltpu.VMEM((576, 128), BF16),
            pltpu.VMEM((32, 256), BF16),
            pltpu.VMEM((32, 256), BF16),
            pltpu.VMEM((1024, 128), BF16),
            pltpu.VMEM((128, 512), BF16),
            pltpu.VMEM((128, 128), BF16),
            pltpu.VMEM((128, 128), BF16),
            pltpu.VMEM((128, 512), BF16),
            pltpu.VMEM((512, 128), BF16),
            pltpu.VMEM((2, 768, 128), F32),
            pltpu.VMEM((1024, 256), BF16),
            pltpu.VMEM((768, 768), BF16),
            pltpu.VMEM((2048, 256), BF16),
            pltpu.VMEM((32, 768), BF16),
            pltpu.VMEM((4, 2, 32, 128), BF16),
            pltpu.VMEM((16, 4, 2, 32, 128), BF16),
            pltpu.VMEM((512, 896), BF16),
            pltpu.VMEM((768, 512), BF16),
            pltpu.VMEM((384, 2048), BF16),
            pltpu.VMEM((576, 128), F32),
            pltpu.VMEM((576, 128), F32),
            pltpu.VMEM((576, 128), BF16),
            pltpu.VMEM((576, 128), F32),
            pltpu.VMEM((576, 128), F32),
            pltpu.VMEM((16, 576, 128), BF16),
            pltpu.VMEM((576, 128), BF16),
            pltpu.VMEM((4, 4, 4, 144, 128), BF16),
            pltpu.VMEM((4, 4, 576, 128), F32),
            pltpu.VMEM((4, 144, 128), F32),
            pltpu.VMEM((4608, 128), F32),
            pltpu.SemaphoreType.DMA((TRANSFERS,)),
            pltpu.SemaphoreType.DMA((TRANSFERS,)),
            pltpu.SemaphoreType.DMA((12,)),
        ],
        compiler_params=pltpu.CompilerParams(
            collective_id=0, has_side_effects=True, vmem_limit_bytes=60 * 1024 * 1024
        ),
        cost_estimate=pl.CostEstimate(
            flops=1_500_000_000, bytes_accessed=2_000_000, transcendentals=400_000
        ),
    )(
        alignment.reshape(768, 256), alignment_mask.T, residue_mask, pair_features.reshape(576, 128),
        weights[0].T, weights[1].T, *weights[2:],
    )
    return out.reshape(24, 24, 128)


def solution(mesh):
    placed = (P("row", "col", None), P("row", "col"), P(), P("row", "col", None)) + (P(),) * 8
    return jax.shard_map(
        shards, mesh=mesh, in_specs=placed, out_specs=P("row", "col", None), check_vma=False
    )
```
